512 devices in a mesh: fsdp: 16 (over z), ctx: 32 (over x, y, core).
Axes of the slice: x: 4, y: 4, z: 16, core: 2. Of those that a mesh axis runs over, the one named last changes fastest.
Arguments:
- queries: bfloat16 [65536, 2048], P(('fsdp', 'ctx')), may hold values from -320 to 320
- keys: bfloat16 [65536, 2048], P(('fsdp', 'ctx')), may hold values from -5 to 5
- values: bfloat16 [65536, 2048], P(('fsdp', 'ctx')), may hold values from -24 to 24
- out_weight: bfloat16 [2048, 2048], P('fsdp'), may hold values from -0.125 to 0.125
- cotangent: bfloat16 [65536, 2048], P(('fsdp', 'ctx')), may hold values from -6 to 6
- positions: int32 [8192], replicated, may hold values from 0 to 65535, as said below
- global_blocks: int32 [2], replicated, may hold values from 0 to 1023
- random_blocks: int32 [1024, 32, 3], P('fsdp', 'ctx'), may hold values from 0 to 1023, as said below
Outputs:
- context: bfloat16 [65536, 2048], P(('fsdp', 'ctx'))
- grad_queries: bfloat16 [65536, 2048], P(('fsdp', 'ctx'))
- grad_keys: bfloat16 [65536, 2048], P(('fsdp', 'ctx'))
- grad_values: bfloat16 [65536, 2048], P(('fsdp', 'ctx'))
The draws below stay inside these ranges and needn't reach their ends.
Inputs may be any that keep to these rules, and one draw needn't show every extreme that they name: random_blocks[i, h, r] lies in the same aligned run of 64 blocks as i. `positions`: the first and the last block of every aligned run of 64 blocks hold at least one listed position.
All inputs are finite; a program needn't handle non-finite values.
Results may differ from the reference program's by a relative error of at most 0.008.
Values may be sent and summed in bfloat16 or wider, within the bound.
A program may use at most 64 MiB of HBM per device.

```python
import math
import jax
import jax.numpy as jnp
from jax import lax

D = 2048
HEADS = 32
HD = 64
BLK = 64
GLOB = 2
RAND = 3
LEN = 65536
NB = 1024
REGION = 64
MASKED = 8192


def paired_draw(key):
    seed_query = jax.random.fold_in(key, 101)
    seed_key = jax.random.fold_in(key, 202)
    dims_all = (LEN, HEADS, HD)
    query_full = jax.random.truncated_normal(seed_query, -4.0, 4.0, dims_all, jnp.float32)
    key_full = jax.random.truncated_normal(seed_key, -4.0, 4.0, dims_all, jnp.float32)
    return (query_full.reshape(LEN, HEADS * HD), key_full.reshape(LEN, HEADS * HD))


def draw_queries(key, part):
    return paired_draw(key)[0].astype(jnp.bfloat16)


def draw_keys(key, part):
    return paired_draw(key)[1].astype(jnp.bfloat16)


def draw_random_blocks(key, part):
    seed_pick = jax.random.fold_in(key, 404)
    start = jnp.arange(NB, dtype=jnp.int32) // REGION * REGION
    offset = jax.random.randint(seed_pick, (NB, HEADS, RAND), 0, REGION, dtype=jnp.int32)
    return (start[:, None, None] + offset).astype(jnp.int32)


def draw_positions(key, part):
    key = jax.random.fold_in(key, 505)
    seed_edge = jax.random.fold_in(key, 1)
    seed_rest = jax.random.fold_in(key, 2)
    region_count = NB // REGION
    index = jnp.arange(MASKED, dtype=jnp.int32)
    inside = jax.random.randint(seed_edge, (MASKED,), 0, BLK, dtype=jnp.int32)
    spread = jax.random.randint(seed_rest, (MASKED,), 0, LEN, dtype=jnp.int32)
    lower = index * REGION * BLK + inside
    upper = ((index - region_count + 1) * REGION - 1) * BLK + inside
    chosen = jnp.where(index < region_count, lower, jnp.where(index < 2 * region_count, upper, spread))
    return chosen.astype(jnp.int32)


def steps_of(rng, dims, split, least, largest):
    def one(dim, blocks):
        draws = jax.random.uniform(jax.random.fold_in(jax.random.fold_in(rng, 6), dim), (blocks,), jnp.float32, least / len(split), largest / len(split))
        return jnp.repeat(jnp.exp(draws), dims[dim] // blocks).reshape((-1,) + (1,) * (len(dims) - dim - 1))

    level = one(*split[0])
    for cut in split[1:]:
        level = level * one(*cut)
    return level


def scatter_about(own_key, shape, scale, bound, split=(), kind=jnp.bfloat16):
    entries = jax.random.normal(own_key, shape, jnp.float32) * scale
    if len(split) > 0:
        entries = steps_of(own_key, shape, split, -0.22, 0.18) * entries
    return jnp.clip(entries, min=-bound, max=bound).astype(kind)


def setup_inputs(seed: int = 0) -> dict:
    key_list = jax.random.split(jax.random.key(seed), 9)
    queries = draw_queries(jax.random.fold_in(key_list[8], 71), 0)
    keys = draw_keys(jax.random.fold_in(key_list[8], 71), 0)
    values = scatter_about(key_list[2], (LEN, D), 4.0, 24.0, ((0, 512),))
    out_weight = scatter_about(key_list[3], (D, D), D ** -0.5, 0.125, ((0, 16),))
    cotangent = scatter_about(key_list[4], (LEN, D), 1.0, 6.0, ((0, 512),))
    positions = draw_positions(jax.random.fold_in(key_list[8], 71), 0)
    global_blocks = jax.random.randint(key_list[6], (GLOB,), 0, NB).astype(jnp.int32)
    random_blocks = draw_random_blocks(jax.random.fold_in(key_list[8], 71), 0)
    return {"queries": queries, "keys": keys, "values": values, "out_weight": out_weight, "cotangent": cotangent, "positions": positions, "global_blocks": global_blocks, "random_blocks": random_blocks}


def slot_table(global_list, random_list):
    block_count = random_list.shape[0]
    head_count = random_list.shape[1]
    current = jnp.arange(block_count, dtype=jnp.int32)
    window = jnp.stack([current - 1, current, current + 1], axis=1)
    window = jnp.broadcast_to(window[:, None, :], (block_count, head_count, 3))
    globals_wide = jnp.broadcast_to(global_list[None, None, :], (block_count, head_count, global_list.shape[0]))
    slot_ids = jnp.concatenate([window, globals_wide.astype(jnp.int32), random_list.astype(jnp.int32)], axis=2)
    slot_count = slot_ids.shape[2]
    inside = (slot_ids >= 0) & (slot_ids < block_count)
    order = jnp.arange(slot_count)
    earlier = order[None, :] < order[:, None]
    repeated = jnp.any((slot_ids[..., :, None] == slot_ids[..., None, :]) & earlier, axis=-1)
    usable = inside & jnp.logical_not(repeated)
    return (jnp.clip(slot_ids, 0, block_count - 1).astype(jnp.int32), usable)

def head_core(query_blocks, key_blocks, value_blocks, grad_blocks, slot_ids, usable):
    block_count = query_blocks.shape[0]
    slot_count = slot_ids.shape[1]
    factor = 1.0 / math.sqrt(HD)
    key_group = key_blocks[slot_ids].reshape(block_count, slot_count * BLK, HD).astype(jnp.float32)
    value_group = value_blocks[slot_ids].reshape(block_count, slot_count * BLK, HD).astype(jnp.float32)
    query_full = query_blocks.astype(jnp.float32)
    grad_full = grad_blocks.astype(jnp.float32)
    keymask = jnp.repeat(usable, BLK, axis=1)[:, None, :]
    scores = jnp.einsum('nqd,nkd->nqk', query_full, key_group) * factor
    scores = jnp.where(keymask, scores, -1e+30)
    highest = lax.optimization_barrier(jnp.max(scores, axis=-1, keepdims=True))
    raised = jnp.where(keymask, jnp.exp(scores - highest), 0.0)
    probs = raised / lax.optimization_barrier(jnp.sum(raised, axis=-1, keepdims=True))
    probs_half = lax.optimization_barrier(probs.astype(jnp.bfloat16))
    context = jnp.einsum('nqk,nkd->nqd', probs_half.astype(jnp.float32), value_group).astype(jnp.bfloat16)
    grad_probs = jnp.einsum('nqd,nkd->nqk', grad_full, value_group)
    inner = lax.optimization_barrier(jnp.sum(probs * grad_probs, axis=-1, keepdims=True))
    grad_scores = lax.optimization_barrier((probs * (grad_probs - inner) * factor).astype(jnp.bfloat16))
    grad_query = jnp.einsum('nqk,nkd->nqd', grad_scores.astype(jnp.float32), key_group).astype(jnp.bfloat16)
    key_terms = jnp.einsum('nqk,nqd->nkd', grad_scores.astype(jnp.float32), query_full)
    value_terms = jnp.einsum('nqk,nqd->nkd', probs_half.astype(jnp.float32), grad_full)
    key_terms = key_terms.reshape(block_count * slot_count, BLK, HD)
    value_terms = value_terms.reshape(block_count * slot_count, BLK, HD)
    targets = jnp.where(usable, slot_ids, block_count).reshape(-1).astype(jnp.int32)
    grad_key = jax.ops.segment_sum(key_terms, targets, num_segments=block_count + 1)[:block_count]
    grad_value = jax.ops.segment_sum(value_terms, targets, num_segments=block_count + 1)[:block_count]
    return (context, grad_query, grad_key.astype(jnp.bfloat16), grad_value.astype(jnp.bfloat16))

def run_head(packed):
    return head_core(packed[0], packed[1], packed[2], packed[3], packed[4], packed[5])

def reference(queries, keys, values, out_weight, cotangent, positions, global_blocks, random_blocks):
    block_count = LEN // BLK

    def to_heads(rows):
        return rows.reshape(block_count, BLK, HEADS, HD).transpose(2, 0, 1, 3)

    def from_heads(blocks):
        return blocks.transpose(1, 2, 0, 3).reshape(LEN, HEADS * HD)
    masked = jnp.zeros((LEN,), jnp.int32).at[positions.astype(jnp.int32)].set(1) > 0
    upstream = jnp.where(masked[:, None], cotangent, jnp.zeros_like(cotangent))
    grad_context = jnp.dot(upstream, out_weight.T, preferred_element_type=jnp.float32).astype(jnp.bfloat16)
    slot_ids, usable = slot_table(global_blocks, random_blocks)
    results = lax.map(run_head, (to_heads(queries), to_heads(keys), to_heads(values), to_heads(grad_context), slot_ids.transpose(1, 0, 2), usable.transpose(1, 0, 2)))
    return (from_heads(results[0]), from_heads(results[1]), from_heads(results[2]), from_heads(results[3]))
```

```python
import functools
import math

import jax
import jax.numpy as jnp
from jax import lax
from jax.experimental import pallas as pl
from jax.experimental.pallas import tpu as pltpu
from jax.sharding import PartitionSpec as P

HD = 64
BLK = 64
GLOB = 2
SLOTS = 8


def contract(a, b, da, db):
    return lax.dot_general(a, b, (((da,), (db,)), ((), ())), preferred_element_type=jnp.float32)


def attend_kernel(pairs, ids_ref, kv_ref, qg_ref, bias_ref, dqo_ref, dkv_ref):
    width = 2 * HD
    scale = math.log2(math.e) / math.sqrt(HD)
    low = lax.broadcasted_iota(jnp.int32, (BLK, width), 1) < HD
    zero = jnp.zeros((BLK, width), jnp.bfloat16)
    dkv_ref[...] = jnp.zeros_like(dkv_ref)
    blocks = kv_ref.shape[0] // BLK

    def rows(block):
        return pl.ds(pl.multiple_of(block * BLK, BLK), BLK)

    def step(j, carry):
        first = qg_ref[rows(2 * j), :]
        second = qg_ref[rows(2 * j + 1), :]
        mixed = jnp.concatenate(
            [
                jnp.concatenate([jnp.where(low, first, zero), zero], axis=1),
                jnp.concatenate([zero, jnp.where(low, second, zero)], axis=1),
                jnp.concatenate([jnp.where(low, zero, first), zero], axis=1),
                jnp.concatenate([zero, jnp.where(low, zero, second)], axis=1),
            ],
            axis=0,
        )
        left = [ids_ref[2 * j, s] for s in range(SLOTS)]
        right = [ids_ref[2 * j + 1, s] for s in range(SLOTS)]
        both = jnp.concatenate(
            [
                jnp.concatenate([kv_ref[rows(a), :], kv_ref[rows(b), :]], axis=1)
                for a, b in zip(left, right)
            ],
            axis=0,
        )
        products = contract(both, mixed, 1, 1)
        scores = []
        for s in range(SLOTS):
            part = products[s * BLK : (s + 1) * BLK, :width]
            scores.append(part * scale + bias_ref[pl.ds(j * SLOTS + s, 1), :])
        highest = functools.reduce(jnp.maximum, scores)
        highest = jnp.max(highest, axis=0, keepdims=True)
        raised = [jnp.exp2(part - highest) for part in scores]
        total = jnp.sum(functools.reduce(jnp.add, raised), axis=0, keepdims=True)
        inverse = 1.0 / total
        probs = [part * inverse for part in raised]
        grads = [products[s * BLK : (s + 1) * BLK, width:] for s in range(SLOTS)]
        inner = functools.reduce(jnp.add, [p * g for p, g in zip(probs, grads)])
        inner = jnp.sum(inner, axis=0, keepdims=True)
        weights = jnp.concatenate(
            [
                jnp.concatenate(
                    [(p * (g - inner)).astype(jnp.bfloat16), p.astype(jnp.bfloat16)], axis=1
                )
                for p, g in zip(probs, grads)
            ],
            axis=0,
        )
        sums = contract(weights, both, 0, 0)
        eighth = jnp.where(low, 1.0 / math.sqrt(HD), 1.0)
        out_first = jnp.where(low, sums[:BLK, :width], sums[2 * BLK : 3 * BLK, :width]) * eighth
        out_second = jnp.where(low, sums[BLK : 2 * BLK, width:], sums[3 * BLK :, width:]) * eighth
        dqo_ref[rows(2 * j), :] = out_first.astype(jnp.bfloat16)
        dqo_ref[rows(2 * j + 1), :] = out_second.astype(jnp.bfloat16)
        terms = contract(weights, mixed, 1, 0)

        def term(s, side):
            return terms[s * BLK : (s + 1) * BLK, side * width : (side + 1) * width]

        dkv_ref[rows(2 * j), :] += term(0, 0)
        dkv_ref[rows(2 * j + 1), :] += term(1, 0) + term(0, 1)
        dkv_ref[rows(2 * j + 2), :] += term(2, 0) + term(1, 1)
        dkv_ref[rows(2 * j + 3), :] += term(2, 1)
        for s in range(3, 3 + GLOB):
            dkv_ref[rows(blocks - GLOB + s - 3), :] += term(s, 0) + term(s, 1)
        for s in range(3 + GLOB, SLOTS):
            dkv_ref[rows(left[s]), :] += term(s, 0)
            dkv_ref[rows(right[s]), :] += term(s, 1)
        return carry

    lax.fori_loop(0, pairs, step, 0)
    eighth = jnp.where(low, 1.0 / math.sqrt(HD), 1.0)

    def finish(b, carry):
        dkv_ref[rows(b), :] = dkv_ref[rows(b), :] * eighth
        return carry

    lax.fori_loop(0, blocks, finish, 0)


def attend(ids, kv, qg, bias):
    pairs = qg.shape[0] // (2 * BLK)
    vmem = pl.BlockSpec(memory_space=pltpu.VMEM)
    return pl.pallas_call(
        functools.partial(attend_kernel, pairs),
        out_shape=(
            jax.ShapeDtypeStruct(qg.shape, jnp.bfloat16),
            jax.ShapeDtypeStruct(kv.shape, jnp.float32),
        ),
        in_specs=[pl.BlockSpec(memory_space=pltpu.SMEM), vmem, vmem, vmem],
        out_specs=(vmem, vmem),
        compiler_params=pltpu.CompilerParams(vmem_limit_bytes=48 * 1024 * 1024),
    )(ids, kv, qg, bias)


def neighbours(block, dim, width):
    count = lax.axis_size("fsdp")
    forward = [(i, i + 1) for i in range(count - 1)]
    backward = [(target, source) for source, target in forward]
    last = lax.slice_in_dim(block, block.shape[dim] - width, None, axis=dim)
    low = lax.ppermute(last, "fsdp", forward)
    high = lax.ppermute(lax.slice_in_dim(block, 0, width, axis=dim), "fsdp", backward)
    return low, high


def pack(a, b):
    heads = a.shape[1] // HD
    both = jnp.stack([a.reshape(-1, heads, HD), b.reshape(-1, heads, HD)], axis=2)
    return both.reshape(a.shape[0], 2 * a.shape[1])


def unpack(both):
    heads = both.shape[1] // (2 * HD)
    split = both.reshape(-1, heads, 2, HD)
    return split[:, :, 0].reshape(-1, heads * HD), split[:, :, 1].reshape(-1, heads * HD)


def tables(global_blocks, random_blocks, local_blocks):
    group = lax.axis_index("fsdp")
    first_block = group * local_blocks
    block_total = local_blocks * lax.axis_size("fsdp")
    local_ids = jnp.arange(local_blocks, dtype=jnp.int32)
    current = first_block + local_ids
    window = jnp.stack([current - 1, current, current + 1], axis=1)
    globals_wide = jnp.broadcast_to(global_blocks[None, :], (local_blocks, GLOB))
    slot_ids = jnp.concatenate([window, globals_wide, random_blocks], axis=1)
    inside = (slot_ids >= 0) & (slot_ids < block_total)
    order = jnp.arange(SLOTS)
    earlier = order[None, :] < order[:, None]
    repeated = jnp.any((slot_ids[:, :, None] == slot_ids[:, None, :]) & earlier, axis=-1)
    usable = inside & jnp.logical_not(repeated)
    near = jnp.stack([local_ids, local_ids + 1, local_ids + 2], axis=1)
    far = local_blocks + 2 + jnp.arange(GLOB, dtype=jnp.int32)
    far = jnp.broadcast_to(far[None, :], (local_blocks, GLOB))
    ids = jnp.concatenate([near, far, random_blocks - first_block + 1], axis=1)
    bias = jnp.where(usable, 0.0, -1e30).astype(jnp.float32)
    bias = bias.reshape(local_blocks // 2, 2, SLOTS).transpose(0, 2, 1)
    bias = jnp.repeat(bias.reshape(-1, 2), BLK, axis=1)
    return ids, bias


def body(queries, keys, values, out_weight, cotangent, positions, global_blocks, random_blocks):
    rows_here = queries.shape[0]
    offset = (lax.axis_index("fsdp") * lax.axis_size("ctx") + lax.axis_index("ctx")) * rows_here
    places = offset + jnp.arange(rows_here, dtype=jnp.int32)
    masked = jnp.any(positions[:, None] == places[None, :], axis=0)
    upstream = jnp.where(masked[:, None], cotangent, jnp.zeros_like(cotangent))
    grad_context = contract(
        upstream, lax.all_gather(out_weight, "fsdp", axis=0, tiled=True), 1, 1
    ).astype(jnp.bfloat16)
    kv = lax.all_to_all(pack(keys, values), "ctx", split_axis=1, concat_axis=0, tiled=True)
    qg = lax.all_to_all(pack(queries, grad_context), "ctx", split_axis=1, concat_axis=0, tiled=True)
    seg_len = kv.shape[0]
    local_blocks = seg_len // BLK
    group = lax.axis_index("fsdp")
    low, high = neighbours(kv, 0, BLK)
    owner = global_blocks // local_blocks
    spot = global_blocks % local_blocks
    picks = []
    for which in range(GLOB):
        piece = lax.dynamic_slice_in_dim(kv, spot[which] * BLK, BLK, 0)
        picks.append(jnp.where(owner[which] == group, piece, jnp.zeros_like(piece)))
    shared = lax.psum(jnp.concatenate(picks, axis=0), "fsdp")
    ids, bias = tables(global_blocks, random_blocks[:, 0], local_blocks)
    dqo, sums = attend(ids, jnp.concatenate([low, kv, high, shared], axis=0), qg, bias)
    edges = jnp.concatenate([sums[:BLK], sums[BLK + seg_len : 2 * BLK + seg_len]], axis=0)
    from_low, from_high = neighbours(edges, 0, BLK)
    local = sums[BLK : BLK + seg_len]
    local = local.at[:BLK].add(from_low)
    local = local.at[seg_len - BLK :].add(from_high)
    global_sums = lax.psum(sums[2 * BLK + seg_len :], "fsdp")
    for which in range(GLOB):
        term = global_sums[which * BLK : (which + 1) * BLK]
        term = jnp.where(owner[which] == group, term, jnp.zeros_like(term))
        begin = spot[which] * BLK
        current = lax.dynamic_slice_in_dim(local, begin, BLK, 0)
        local = lax.dynamic_update_slice_in_dim(local, current + term, begin, 0)
    dkv = local.astype(jnp.bfloat16)
    grad_query, context = unpack(lax.all_to_all(dqo, "ctx", split_axis=0, concat_axis=1, tiled=True))
    grad_key, grad_value = unpack(
        lax.all_to_all(dkv, "ctx", split_axis=0, concat_axis=1, tiled=True)
    )
    return (context, grad_query, grad_key, grad_value)


def solution(mesh):
    split = P(("fsdp", "ctx"), None)
    return jax.shard_map(
        body,
        mesh=mesh,
        in_specs=(split, split, split, P("fsdp", None), split, P(), P(), P("fsdp", "ctx", None)),
        out_specs=(split, split, split, split),
        check_vma=False,
    )
```

```python
import functools
import math

import jax
import jax.numpy as jnp
from jax import lax
from jax.experimental import pallas as pl
from jax.experimental.pallas import tpu as pltpu
from jax.sharding import PartitionSpec as P

HD = 64
BLK = 64
GLOB = 2
SLOTS = 8


def contract(a, b, da, db):
    return lax.dot_general(a, b, (((da,), (db,)), ((), ())), preferred_element_type=jnp.float32)


def attend_kernel(pairs, ids_ref, kv_ref, qg_ref, bias_ref, dqo_ref, dkv_ref):
    width = 2 * HD
    scale = math.log2(math.e) / math.sqrt(HD)
    low = lax.broadcasted_iota(jnp.int32, (BLK, width), 1) < HD
    zero = jnp.zeros((BLK, width), jnp.bfloat16)
    dkv_ref[...] = jnp.zeros_like(dkv_ref)
    blocks = kv_ref.shape[0] // BLK

    def rows(block):
        return pl.ds(pl.multiple_of(block * BLK, BLK), BLK)

    def step(j, carry):
        first = qg_ref[rows(2 * j), :]
        second = qg_ref[rows(2 * j + 1), :]
        mixed = jnp.concatenate(
            [
                jnp.concatenate([jnp.where(low, first, zero), zero], axis=1),
                jnp.concatenate([zero, jnp.where(low, second, zero)], axis=1),
                jnp.concatenate([jnp.where(low, zero, first), zero], axis=1),
                jnp.concatenate([zero, jnp.where(low, zero, second)], axis=1),
            ],
            axis=0,
        )
        left = [ids_ref[2 * j, s] for s in range(SLOTS)]
        right = [ids_ref[2 * j + 1, s] for s in range(SLOTS)]
        both = jnp.concatenate(
            [
                jnp.concatenate([kv_ref[rows(a), :], kv_ref[rows(b), :]], axis=1)
                for a, b in zip(left, right)
            ],
            axis=0,
        )
        products = contract(both, mixed, 1, 1)
        scores = []
        for s in range(SLOTS):
            part = products[s * BLK : (s + 1) * BLK, :width]
            scores.append(part * scale + bias_ref[pl.ds(j * SLOTS + s, 1), :])
        highest = functools.reduce(jnp.maximum, scores)
        highest = jnp.max(highest, axis=0, keepdims=True)
        raised = [jnp.exp2(part - highest) for part in scores]
        total = jnp.sum(functools.reduce(jnp.add, raised), axis=0, keepdims=True)
        inverse = 1.0 / total
        probs = [part * inverse for part in raised]
        grads = [products[s * BLK : (s + 1) * BLK, width:] for s in range(SLOTS)]
        inner = functools.reduce(jnp.add, [p * g for p, g in zip(probs, grads)])
        inner = jnp.sum(inner, axis=0, keepdims=True)
        weights = jnp.concatenate(
            [
                jnp.concatenate(
                    [(p * (g - inner)).astype(jnp.bfloat16), p.astype(jnp.bfloat16)], axis=1
                )
                for p, g in zip(probs, grads)
            ],
            axis=0,
        )
        sums = contract(weights, both, 0, 0)
        eighth = jnp.where(low, 1.0 / math.sqrt(HD), 1.0)
        out_first = jnp.where(low, sums[:BLK, :width], sums[2 * BLK : 3 * BLK, :width]) * eighth
        out_second = jnp.where(low, sums[BLK : 2 * BLK, width:], sums[3 * BLK :, width:]) * eighth
        dqo_ref[rows(2 * j), :] = out_first.astype(jnp.bfloat16)
        dqo_ref[rows(2 * j + 1), :] = out_second.astype(jnp.bfloat16)
        terms = contract(weights, mixed, 1, 0)

        def term(s, side):
            return terms[s * BLK : (s + 1) * BLK, side * width : (side + 1) * width]

        dkv_ref[rows(2 * j), :] += term(0, 0)
        dkv_ref[rows(2 * j + 1), :] += term(1, 0) + term(0, 1)
        dkv_ref[rows(2 * j + 2), :] += term(2, 0) + term(1, 1)
        dkv_ref[rows(2 * j + 3), :] += term(2, 1)
        for s in range(3, 3 + GLOB):
            dkv_ref[rows(blocks - GLOB + s - 3), :] += term(s, 0) + term(s, 1)
        for s in range(3 + GLOB, SLOTS):
            dkv_ref[rows(left[s]), :] += term(s, 0)
            dkv_ref[rows(right[s]), :] += term(s, 1)
        return carry

    lax.fori_loop(0, pairs, step, 0)
    eighth = jnp.where(low, 1.0 / math.sqrt(HD), 1.0)

    def finish(b, carry):
        dkv_ref[rows(b), :] = dkv_ref[rows(b), :] * eighth
        return carry

    lax.fori_loop(0, blocks, finish, 0)


def attend(ids, kv, qg, bias):
    pairs = qg.shape[0] // (2 * BLK)
    vmem = pl.BlockSpec(memory_space=pltpu.VMEM)
    return pl.pallas_call(
        functools.partial(attend_kernel, pairs),
        out_shape=(
            jax.ShapeDtypeStruct(qg.shape, jnp.bfloat16),
            jax.ShapeDtypeStruct(kv.shape, jnp.float32),
        ),
        in_specs=[pl.BlockSpec(memory_space=pltpu.SMEM), vmem, vmem, vmem],
        out_specs=(vmem, vmem),
        compiler_params=pltpu.CompilerParams(vmem_limit_bytes=48 * 1024 * 1024),
    )(ids, kv, qg, bias)


CAP = 32
MESH = pl.DeviceIdType.MESH


def place(nz, nctx):
    z = lax.axis_index("fsdp")
    c = lax.axis_index("ctx")
    return z, c


def greet(nz, nctx):
    z, c = place(nz, nctx)
    barrier = pltpu.get_barrier_semaphore()

    def plane(d, carry):
        peer = lax.rem(c + d, nctx)
        pl.semaphore_signal(barrier, inc=1, device_id=(z, peer), device_id_type=MESH)
        return carry

    def column(d, carry):
        peer = lax.rem(z + d, nz)
        pl.semaphore_signal(barrier, inc=1, device_id=(peer, c), device_id_type=MESH)
        return carry

    lax.fori_loop(1, nctx, plane, 0)
    lax.fori_loop(1, nz, column, 0)
    pl.semaphore_wait(barrier, nctx + nz - 2)


def plane_copy(nz, nctx, d, src, dst, send, recv, incoming=False):
    z, c = place(nz, nctx)
    peer = lax.rem(c + d, nctx)
    source = lax.rem(c - d + nctx, nctx) if incoming else c
    return pltpu.make_async_remote_copy(
        src_ref=src(peer),
        dst_ref=dst(source),
        send_sem=send.at[d],
        recv_sem=recv.at[d],
        device_id=(z, peer),
        device_id_type=MESH,
    )


def column_copy(peer, src, dst, send, recv):
    c = lax.axis_index("ctx")
    return pltpu.make_async_remote_copy(
        src_ref=src,
        dst_ref=dst,
        send_sem=send,
        recv_sem=recv,
        device_id=(peer, c),
        device_id_type=MESH,
    )


def inner_copies(nz, nctx, side, src, buf, send, recv):
    z, c = place(nz, nctx)
    group, member = z // side, lax.rem(z, side)
    return [
        column_copy(
            group * side + lax.rem(member + e, side), src, buf.at[e], send.at[e], recv.at[e]
        )
        for e in range(1, side)
    ]


def outer_copies(nz, nctx, side, src, buf, send, recv):
    z, c = place(nz, nctx)
    group, member = z // side, lax.rem(z, side)
    groups = nz // side
    return [
        column_copy(
            lax.rem(group + e, groups) * side + member, src, buf.at[e], send.at[e], recv.at[e]
        )
        for e in range(1, groups)
    ]


def edge_copies(nz, down_src, down_dst, up_src, up_dst, send, recv):
    z = lax.axis_index("fsdp")
    down = column_copy(jnp.maximum(z - 1, 0), down_src, down_dst, send.at[0], recv.at[0])
    up = column_copy(jnp.minimum(z + 1, nz - 1), up_src, up_dst, send.at[1], recv.at[1])
    return down, up


def halves(x):
    return jnp.concatenate([x[:, HD:], x[:, :HD]], axis=1)


def chosen(rank_row):
    order = lax.broadcasted_iota(jnp.int32, (CAP, rank_row.shape[1]), 0).astype(jnp.float32)
    return jnp.where(order == rank_row, 1.0, 0.0).astype(jnp.bfloat16)


def collect_kernel(
    nz, nctx, glob_ref, q_ref, k_ref, v_ref, ct_ref, w_ref, pos_ref,
    kv_ref, qg_ref, rank_ref, most_ref,
    kv_pack, q_pack, q_all, up_own, up_all, w_all, g_all, count, g_own, g_in, g_mid, g_out,
    kv_send, kv_recv, q_send, q_recv, up_send, up_recv, w_send, w_recv, a_send, a_recv,
    edge_send, edge_recv, in_send, in_recv, out_send, out_recv, pair_send, pair_recv,
):
    z, c = place(nz, nctx)
    chip, core = c // 2, lax.rem(c, 2)
    rows = q_ref.shape[0]
    wide = q_ref.shape[1]
    side = max(s for s in range(1, nz + 1) if s * s <= nz)
    local_blocks = nctx * rows // BLK
    partner = 2 * chip + 1 - core
    low = lax.broadcasted_iota(jnp.int32, (BLK, 2 * HD), 1) < HD
    greet(nz, nctx)

    piece_rows = 2 * rows // nz

    def piece(ref, i):
        return ref.at[
            pl.ds(pl.multiple_of((i // 2) * piece_rows, piece_rows), piece_rows),
            pl.ds(pl.multiple_of(core * (wide // 2) + lax.rem(i, 2) * (wide // 4), wide // 4), wide // 4),
        ]

    def weight_out(d):
        i = lax.rem(z + d, nz)
        return column_copy(i, piece(w_ref, i), piece(w_all, i), w_send.at[d], w_recv)

    is_source = z == chip

    @pl.when(is_source)
    def _():
        def go(d, carry):
            weight_out(d).start()
            return carry

        lax.fori_loop(1, nz, go, 0)
        w_all[...] = w_ref[...]

    for t in range(nctx // 2):
        k_two = k_ref[:, 2 * t * HD : 2 * (t + 1) * HD]
        v_two = v_ref[:, 2 * t * HD : 2 * (t + 1) * HD]
        kv_pack[2 * t] = jnp.concatenate([k_two[:, :HD], v_two[:, :HD]], axis=1)
        kv_pack[2 * t + 1] = jnp.concatenate([k_two[:, HD:], v_two[:, HD:]], axis=1)

    def kv_rows(source):
        return kv_ref.at[pl.ds(pl.multiple_of(BLK + source * rows, BLK), rows)]

    def kv_copy(d, incoming=False):
        return plane_copy(nz, nctx, d, lambda p: kv_pack.at[p], kv_rows, kv_send, kv_recv, incoming)

    def kv_go(d, carry):
        kv_copy(d).start()
        return carry

    lax.fori_loop(1, nctx, kv_go, 0)
    kv_ref[pl.ds(pl.multiple_of(BLK + c * rows, BLK), rows)] = kv_pack[c]

    for t in range(nctx // 2):
        top = q_ref[:BLK, 2 * t * HD : 2 * (t + 1) * HD]
        bottom = q_ref[BLK:, 2 * t * HD : 2 * (t + 1) * HD]
        q_pack[2 * t] = jnp.concatenate([top[:, :HD], bottom[:, :HD]], axis=1)
        q_pack[2 * t + 1] = jnp.concatenate([top[:, HD:], bottom[:, HD:]], axis=1)

    def q_copy(d, incoming=False):
        return plane_copy(nz, nctx, d, lambda p: q_pack.at[p], lambda s: q_all.at[s], q_send, q_recv, incoming)

    def q_go(d, carry):
        q_copy(d).start()
        return carry

    lax.fori_loop(1, nctx, q_go, 0)
    q_all[c] = q_pack[c]

    def weight_copy(d, incoming=False):
        peer = lax.rem(z + d, nz)
        at = piece(w_all, lax.rem(z - d + nz, nz) if incoming else z)
        return column_copy(peer, at, at, a_send.at[d], a_recv.at[d])

    @pl.when(jnp.logical_not(is_source))
    def _():
        column_copy(z, piece(w_ref, z), piece(w_all, z), w_send.at[0], w_recv).wait_recv()

    def weight_go(d, carry):
        @pl.when(lax.rem(z + d, nz) != chip)
        def _():
            weight_copy(d).start()

        return carry

    lax.fori_loop(1, nz, weight_go, 0)

    devices = nz * nctx
    count[...] = jnp.zeros_like(count)
    span = pos_ref.shape[1]
    group_ids = lax.broadcasted_iota(jnp.int32, (devices, span), 0)
    inside_ids = lax.broadcasted_iota(jnp.int32, (rows, span), 0)

    def tally(i, carry):
        pos = pos_ref[pl.ds(i, 1), :]
        group = pos // rows
        inside = pos - group * rows
        hit = jnp.where(group_ids == group, 1.0, 0.0).astype(jnp.bfloat16)
        spot = jnp.where(inside_ids == inside, 1.0, 0.0).astype(jnp.bfloat16)
        count[...] += contract(hit, spot, 1, 1)
        return carry

    lax.fori_loop(0, pos_ref.shape[0], tally, 0)
    masked = jnp.where(count[...] > 0.5, 1.0, 0.0)
    before = lax.broadcasted_iota(jnp.int32, (rows, rows), 0) < lax.broadcasted_iota(
        jnp.int32, (rows, rows), 1
    )
    rank = contract(masked.astype(jnp.bfloat16), jnp.where(before, 1.0, 0.0).astype(jnp.bfloat16), 1, 0)
    count[...] = jnp.where(masked > 0.5, rank, -1.0)
    most = jnp.max(jnp.max(count[...], axis=0, keepdims=True), axis=1, keepdims=True)
    most_ref[...] = jnp.broadcast_to(most, most_ref.shape)
    rank_ref[...] = count[pl.ds(pl.multiple_of(z * nctx, nctx), nctx), :]
    mine = chosen(rank_ref[pl.ds(c, 1), :])
    up_own[...] = contract(mine, ct_ref[...], 1, 0).astype(jnp.bfloat16)

    def up_copy(d, incoming=False):
        peer = lax.rem(c + 2 * d, nctx)
        source = lax.rem(chip - d + nctx // 2, nctx // 2) if incoming else chip
        return pltpu.make_async_remote_copy(
            src_ref=up_own,
            dst_ref=up_all.at[pl.ds(pl.multiple_of(source * CAP, CAP), CAP)],
            send_sem=up_send.at[d],
            recv_sem=up_recv.at[d],
            device_id=(z, peer),
            device_id_type=MESH,
        )

    def up_go(d, carry):
        up_copy(d).start()
        return carry

    lax.fori_loop(1, nctx // 2, up_go, 0)
    up_all[pl.ds(pl.multiple_of(chip * CAP, CAP), CAP)] = up_own[...]

    def kv_in(d, carry):
        kv_copy(d, True).wait_recv()
        return carry

    lax.fori_loop(1, nctx, kv_in, 0)
    low_edge = kv_ref.at[pl.ds(0, BLK)]
    high_edge = kv_ref.at[pl.ds((local_blocks + 1) * BLK, BLK)]
    down, up = edge_copies(
        nz, kv_ref.at[pl.ds(BLK, BLK)], high_edge, kv_ref.at[pl.ds(local_blocks * BLK, BLK)],
        low_edge, edge_send, edge_recv,
    )

    @pl.when(z > 0)
    def _():
        down.start()

    @pl.when(z < nz - 1)
    def _():
        up.start()

    wanted = [glob_ref[i] - z * local_blocks for i in range(GLOB)]

    def pick(b, totals):
        block = kv_ref[pl.ds(pl.multiple_of(BLK + b * BLK, BLK), BLK), :]
        return tuple(
            jnp.where(jnp.full(block.shape, wanted[i] == b), block, totals[i]) for i in range(GLOB)
        )

    nothing = jnp.zeros((BLK, 2 * HD), jnp.bfloat16)
    picked = lax.fori_loop(0, local_blocks, pick, (nothing,) * GLOB)
    g_own[...] = jnp.concatenate(picked, axis=0)
    stage_in = inner_copies(nz, nctx, side, g_own, g_in, in_send, in_recv)
    for copy in stage_in:
        copy.start()

    half = pl.ds(pl.multiple_of(core * (wide // 2), wide // 2), wide // 2)
    other_half = pl.ds(pl.multiple_of((1 - core) * (wide // 2), wide // 2), wide // 2)

    def pair_copy(src, dst, i):
        return pltpu.make_async_remote_copy(
            src_ref=src,
            dst_ref=dst,
            send_sem=pair_send.at[i],
            recv_sem=pair_recv.at[i],
            device_id=(z, partner),
            device_id_type=MESH,
        )

    cross_out = pair_copy(w_all.at[:, half], w_all.at[:, half], 0)
    cross_in = pair_copy(w_all.at[:, half], w_all.at[:, other_half], 0)

    @pl.when(jnp.logical_not(is_source))
    def _():
        def weight_in(d, carry):
            weight_copy(d, True).wait_recv()
            return carry

        lax.fori_loop(1, nz, weight_in, 0)
        cross_out.start()

    total = g_own[...].astype(jnp.float32)
    for e, copy in enumerate(stage_in):
        copy.wait_recv()
        total = total + g_in[e + 1].astype(jnp.float32)
    g_mid[...] = total.astype(jnp.bfloat16)
    stage_out = outer_copies(nz, nctx, side, g_mid, g_out, out_send, out_recv)
    for copy in stage_out:
        copy.start()

    def up_in(d, carry):
        up_copy(d, True).wait_recv()
        return carry

    lax.fori_loop(1, nctx // 2, up_in, 0)

    @pl.when(jnp.logical_not(is_source))
    def _():
        cross_in.wait_recv()

    g_all[core] = contract(up_all[...], w_all[...], 1, 1).astype(jnp.bfloat16)
    swap_out = pair_copy(g_all.at[core], g_all.at[core], 1)
    swap_in = pair_copy(g_all.at[core], g_all.at[1 - core], 1)
    swap_out.start()

    @pl.when(z > 0)
    def _():
        column_copy(jnp.maximum(z - 1, 0), low_edge, low_edge, edge_send.at[1], edge_recv.at[1]).wait_recv()

    @pl.when(z == 0)
    def _():
        kv_ref[pl.ds(0, BLK), :] = nothing

    @pl.when(z < nz - 1)
    def _():
        column_copy(
            jnp.minimum(z + 1, nz - 1), high_edge, high_edge, edge_send.at[0], edge_recv.at[0]
        ).wait_recv()

    @pl.when(z == nz - 1)
    def _():
        kv_ref[pl.ds((local_blocks + 1) * BLK, BLK), :] = nothing

    total = g_mid[...].astype(jnp.float32)
    for e, copy in enumerate(stage_out):
        copy.wait_recv()
        total = total + g_out[e + 1].astype(jnp.float32)
    kv_ref[pl.ds((local_blocks + 2) * BLK, GLOB * BLK), :] = total.astype(jnp.bfloat16)

    def q_in(d, carry):
        q_copy(d, True).wait_recv()
        return carry

    lax.fori_loop(1, nctx, q_in, 0)
    swap_in.wait_recv()

    def expand(j, carry):
        marks = chosen(rank_ref[pl.ds(j, 1), :])
        compact = g_all[lax.rem(j, 2), pl.ds(pl.multiple_of((j // 2) * CAP, CAP), CAP), :]
        dense = contract(marks, compact, 0, 0).astype(jnp.bfloat16)
        dense = jnp.where(jnp.full(dense.shape, core == 0), halves(dense), dense)
        two = q_all[j]
        begin = pl.multiple_of(j * rows, rows)
        qg_ref[pl.ds(begin, BLK), :] = jnp.where(low, two, dense[:BLK])
        qg_ref[pl.ds(begin + BLK, BLK), :] = jnp.where(low, halves(two), dense[BLK:])
        return carry

    lax.fori_loop(0, nctx, expand, 0)

    def left_plane(d, carry):
        kv_copy(d).wait_send()
        q_copy(d).wait_send()
        return carry

    lax.fori_loop(1, nctx, left_plane, 0)

    def left_up(d, carry):
        up_copy(d).wait_send()
        return carry

    lax.fori_loop(1, nctx // 2, left_up, 0)

    def left_weight(d, carry):
        @pl.when(lax.rem(z + d, nz) != chip)
        def _():
            weight_copy(d).wait_send()

        @pl.when(is_source)
        def _():
            weight_out(d).wait_send()

        return carry

    lax.fori_loop(1, nz, left_weight, 0)

    @pl.when(z > 0)
    def _():
        down.wait_send()

    @pl.when(z < nz - 1)
    def _():
        up.wait_send()

    for copy in stage_in + stage_out:
        copy.wait_send()

    @pl.when(jnp.logical_not(is_source))
    def _():
        cross_out.wait_send()

    swap_out.wait_send()


def collect(nz, nctx, global_blocks, q, k, v, ct, w, positions):
    rows, wide = q.shape
    region = nctx * rows
    side = max(s for s in range(1, nz + 1) if s * s <= nz)
    half = jnp.bfloat16
    dma = pltpu.SemaphoreType.DMA
    vmem = pl.BlockSpec(memory_space=pltpu.VMEM)
    span = 256
    return pl.pallas_call(
        functools.partial(collect_kernel, nz, nctx),
        out_shape=(
            jax.ShapeDtypeStruct((region + (2 + GLOB) * BLK, 2 * HD), half),
            jax.ShapeDtypeStruct((region, 2 * HD), half),
            jax.ShapeDtypeStruct((nctx, rows), jnp.float32),
            jax.ShapeDtypeStruct((8, 128), jnp.float32),
        ),
        in_specs=[pl.BlockSpec(memory_space=pltpu.SMEM)] + [vmem] * 6,
        out_specs=(vmem,) * 4,
        scratch_shapes=[
            pltpu.VMEM((nctx, rows, 2 * HD), half),
            pltpu.VMEM((nctx, BLK, 2 * HD), half),
            pltpu.VMEM((nctx, BLK, 2 * HD), half),
            pltpu.VMEM((CAP, wide), half),
            pltpu.VMEM((nctx // 2 * CAP, wide), half),
            pltpu.VMEM((rows, wide), half),
            pltpu.VMEM((2, nctx // 2 * CAP, 2 * HD), half),
            pltpu.VMEM((nz * nctx, rows), jnp.float32),
            pltpu.VMEM((GLOB * BLK, 2 * HD), half),
            pltpu.VMEM((side, GLOB * BLK, 2 * HD), half),
            pltpu.VMEM((GLOB * BLK, 2 * HD), half),
            pltpu.VMEM((nz // side, GLOB * BLK, 2 * HD), half),
            dma((nctx,)), dma((nctx,)), dma((nctx,)), dma((nctx,)),
            dma((nctx // 2,)), dma((nctx // 2,)),
            dma((nz,)), dma(()), dma((nz,)), dma((nz,)),
            dma((2,)), dma((2,)),
            dma((side,)), dma((side,)), dma((nz // side,)), dma((nz // side,)),
            dma((2,)), dma((2,)),
        ],
        compiler_params=pltpu.CompilerParams(
            collective_id=0, has_side_effects=True, vmem_limit_bytes=56 * 1024 * 1024
        ),
    )(global_blocks, q, k, v, ct, w, positions.reshape(-1, span))


def deliver_kernel(
    nz, nctx, glob_ref, dqo_ref, sums_ref, rank_ref,
    o_ref, dq_ref, dk_ref, dv_ref,
    oq_pack, oq_all, kv_pack, kv_all, compact, edge_out, edge_in, g_own, g_in, g_mid, g_out,
    oq_send, oq_recv, kv_send, kv_recv, edge_send, edge_recv, in_send, in_recv, out_send, out_recv,
):
    z, c = place(nz, nctx)
    rows = o_ref.shape[0]
    side = max(s for s in range(1, nz + 1) if s * s <= nz)
    local_blocks = nctx * rows // BLK
    few = CAP // 2
    high_begin = (local_blocks + 1) * BLK
    greet(nz, nctx)
    edge_out[0] = sums_ref[pl.ds(0, BLK), :]
    edge_out[1] = sums_ref[pl.ds(high_begin, BLK), :]
    down, up = edge_copies(
        nz, edge_out.at[0], edge_in.at[0], edge_out.at[1], edge_in.at[1], edge_send, edge_recv
    )

    @pl.when(z > 0)
    def _():
        down.start()

    @pl.when(z < nz - 1)
    def _():
        up.start()

    g_own[...] = sums_ref[pl.ds(high_begin + BLK, GLOB * BLK), :].astype(jnp.bfloat16)
    stage_in = inner_copies(nz, nctx, side, g_own, g_in, in_send, in_recv)
    for copy in stage_in:
        copy.start()

    def shrink(j, carry):
        both = dqo_ref[pl.ds(pl.multiple_of(j * rows, rows), rows), :]
        oq_pack[j, pl.ds(0, BLK), :] = jnp.concatenate([both[:BLK, HD:], both[BLK:, HD:]], axis=1)
        picked = contract(chosen(rank_ref[pl.ds(j, 1), :]), both, 1, 0).astype(jnp.bfloat16)
        oq_pack[j, pl.ds(BLK, few), :] = jnp.concatenate([picked[:few, :HD], picked[few:, :HD]], axis=1)
        return carry

    lax.fori_loop(0, nctx, shrink, 0)

    def oq_copy(d, incoming=False):
        return plane_copy(
            nz, nctx, d, lambda p: oq_pack.at[p], lambda s: oq_all.at[s], oq_send, oq_recv, incoming
        )

    def oq_go(d, carry):
        oq_copy(d).start()
        return carry

    lax.fori_loop(1, nctx, oq_go, 0)
    oq_all[c] = oq_pack[c]

    total = g_own[...].astype(jnp.float32)
    for e, copy in enumerate(stage_in):
        copy.wait_recv()
        total = total + g_in[e + 1].astype(jnp.float32)
    g_mid[...] = total.astype(jnp.bfloat16)
    stage_out = outer_copies(nz, nctx, side, g_mid, g_out, out_send, out_recv)
    for copy in stage_out:
        copy.start()

    @pl.when(z > 0)
    def _():
        column_copy(
            jnp.maximum(z - 1, 0), edge_out.at[1], edge_in.at[1], edge_send.at[1], edge_recv.at[1]
        ).wait_recv()

    @pl.when(z == 0)
    def _():
        edge_in[1] = jnp.zeros_like(edge_in[1])

    @pl.when(z < nz - 1)
    def _():
        column_copy(
            jnp.minimum(z + 1, nz - 1), edge_out.at[0], edge_in.at[0], edge_send.at[0], edge_recv.at[0]
        ).wait_recv()

    @pl.when(z == nz - 1)
    def _():
        edge_in[0] = jnp.zeros_like(edge_in[0])

    for copy in stage_out:
        copy.wait_recv()
    for e in range(1, nz // side):
        total = total + g_out[e].astype(jnp.float32)
    wanted = [glob_ref[i] - z * local_blocks for i in range(GLOB)]

    def settle(j, carry):
        for side_of in range(2):
            b = 2 * j + side_of
            term = sums_ref[pl.ds(pl.multiple_of((b + 1) * BLK, BLK), BLK), :]
            for i in range(GLOB):
                extra = total[i * BLK : (i + 1) * BLK]
                term = term + jnp.where(jnp.full(extra.shape, wanted[i] == b), extra, 0.0)
            edge = edge_in[1 - side_of]
            at_edge = j == (nctx - 1) * side_of
            term = term + jnp.where(jnp.full(edge.shape, at_edge), edge, 0.0)
            kv_pack[j, pl.ds(side_of * BLK, BLK), :] = term.astype(jnp.bfloat16)
        return carry

    lax.fori_loop(0, nctx, settle, 0)

    def kv_copy(d, incoming=False):
        return plane_copy(
            nz, nctx, d, lambda p: kv_pack.at[p], lambda s: kv_all.at[s], kv_send, kv_recv, incoming
        )

    def kv_go(d, carry):
        kv_copy(d).start()
        return carry

    lax.fori_loop(1, nctx, kv_go, 0)
    kv_all[c] = kv_pack[c]

    def oq_in(d, carry):
        oq_copy(d, True).wait_recv()
        return carry

    lax.fori_loop(1, nctx, oq_in, 0)
    for t in range(nctx // 2):
        columns = slice(2 * t * HD, 2 * (t + 1) * HD)
        first, second = oq_all[2 * t], oq_all[2 * t + 1]
        o_ref[:BLK, columns] = jnp.concatenate([first[:BLK, :HD], second[:BLK, :HD]], axis=1)
        o_ref[BLK:, columns] = jnp.concatenate([first[:BLK, HD:], second[:BLK, HD:]], axis=1)
        compact[:few, columns] = jnp.concatenate([first[BLK:, :HD], second[BLK:, :HD]], axis=1)
        compact[few:, columns] = jnp.concatenate([first[BLK:, HD:], second[BLK:, HD:]], axis=1)
    marks = chosen(rank_ref[pl.ds(c, 1), :])
    dq_ref[...] = contract(marks, compact[...], 0, 0).astype(jnp.bfloat16)

    def kv_in(d, carry):
        kv_copy(d, True).wait_recv()
        return carry

    lax.fori_loop(1, nctx, kv_in, 0)
    for t in range(nctx // 2):
        columns = slice(2 * t * HD, 2 * (t + 1) * HD)
        first, second = kv_all[2 * t], kv_all[2 * t + 1]
        dk_ref[:, columns] = jnp.concatenate([first[:, :HD], second[:, :HD]], axis=1)
        dv_ref[:, columns] = jnp.concatenate([first[:, HD:], second[:, HD:]], axis=1)

    def left_plane(d, carry):
        oq_copy(d).wait_send()
        kv_copy(d).wait_send()
        return carry

    lax.fori_loop(1, nctx, left_plane, 0)

    @pl.when(z > 0)
    def _():
        down.wait_send()

    @pl.when(z < nz - 1)
    def _():
        up.wait_send()

    for copy in stage_in + stage_out:
        copy.wait_send()


def deliver(nz, nctx, rows, global_blocks, dqo, sums, rank):
    side = max(s for s in range(1, nz + 1) if s * s <= nz)
    half = jnp.bfloat16
    dma = pltpu.SemaphoreType.DMA
    vmem = pl.BlockSpec(memory_space=pltpu.VMEM)
    wide = nctx * HD
    return pl.pallas_call(
        functools.partial(deliver_kernel, nz, nctx),
        out_shape=(jax.ShapeDtypeStruct((rows, wide), half),) * 4,
        in_specs=[pl.BlockSpec(memory_space=pltpu.SMEM)] + [vmem] * 3,
        out_specs=(vmem,) * 4,
        scratch_shapes=[
            pltpu.VMEM((nctx, BLK + CAP // 2, 2 * HD), half),
            pltpu.VMEM((nctx, BLK + CAP // 2, 2 * HD), half),
            pltpu.VMEM((nctx, rows, 2 * HD), half),
            pltpu.VMEM((nctx, rows, 2 * HD), half),
            pltpu.VMEM((CAP, wide), half),
            pltpu.VMEM((2, BLK, 2 * HD), jnp.float32),
            pltpu.VMEM((2, BLK, 2 * HD), jnp.float32),
            pltpu.VMEM((GLOB * BLK, 2 * HD), half),
            pltpu.VMEM((side, GLOB * BLK, 2 * HD), half),
            pltpu.VMEM((GLOB * BLK, 2 * HD), half),
            pltpu.VMEM((nz // side, GLOB * BLK, 2 * HD), half),
            dma((nctx,)), dma((nctx,)), dma((nctx,)), dma((nctx,)),
            dma((2,)), dma((2,)),
            dma((side,)), dma((side,)), dma((nz // side,)), dma((nz // side,)),
        ],
        compiler_params=pltpu.CompilerParams(
            collective_id=1, has_side_effects=True, vmem_limit_bytes=56 * 1024 * 1024
        ),
    )(global_blocks, dqo, sums, rank)


def tables(global_blocks, random_blocks, local_blocks):
    group = lax.axis_index("fsdp")
    first_block = group * local_blocks
    block_total = local_blocks * lax.axis_size("fsdp")
    local_ids = jnp.arange(local_blocks, dtype=jnp.int32)
    current = first_block + local_ids
    window = jnp.stack([current - 1, current, current + 1], axis=1)
    globals_wide = jnp.broadcast_to(global_blocks[None, :], (local_blocks, GLOB))
    slot_ids = jnp.concatenate([window, globals_wide, random_blocks], axis=1)
    inside = (slot_ids >= 0) & (slot_ids < block_total)
    order = jnp.arange(SLOTS)
    earlier = order[None, :] < order[:, None]
    repeated = jnp.any((slot_ids[:, :, None] == slot_ids[:, None, :]) & earlier, axis=-1)
    usable = inside & jnp.logical_not(repeated)
    near = jnp.stack([local_ids, local_ids + 1, local_ids + 2], axis=1)
    far = local_blocks + 2 + jnp.arange(GLOB, dtype=jnp.int32)
    far = jnp.broadcast_to(far[None, :], (local_blocks, GLOB))
    ids = jnp.concatenate([near, far, random_blocks - first_block + 1], axis=1)
    bias = jnp.where(usable, 0.0, -1e30).astype(jnp.float32)
    bias = bias.reshape(local_blocks // 2, 2, SLOTS).transpose(0, 2, 1)
    bias = jnp.repeat(bias.reshape(-1, 2), BLK, axis=1)
    return ids, bias


def body(queries, keys, values, out_weight, cotangent, positions, global_blocks, random_blocks):
    rows_here = queries.shape[0]
    nz, nctx = lax.axis_size("fsdp"), lax.axis_size("ctx")
    local_blocks = nctx * rows_here // BLK
    kv, qg, rank, most = collect(
        nz, nctx, global_blocks, queries, keys, values, cotangent, out_weight, positions
    )
    crowded = most[0, 0] > CAP - 0.5

    def dense_gradient(qg):
        offset = (lax.axis_index("fsdp") * nctx + lax.axis_index("ctx")) * rows_here
        places = offset + jnp.arange(rows_here, dtype=jnp.int32)
        masked = jnp.any(positions[:, None] == places[None, :], axis=0)
        upstream = jnp.where(masked[:, None], cotangent, jnp.zeros_like(cotangent))
        weight = lax.all_gather(out_weight, "fsdp", axis=0, tiled=True)
        grad = contract(upstream, weight, 1, 1).astype(jnp.bfloat16)
        grad = lax.all_to_all(grad, "ctx", split_axis=1, concat_axis=0, tiled=True)
        return jnp.concatenate([qg[:, :HD], grad], axis=1)

    qg = lax.cond(crowded, dense_gradient, lambda qg: qg, qg)
    ids, bias = tables(global_blocks, random_blocks[:, 0], local_blocks)
    dqo, sums = attend(ids, kv, qg, bias)
    context, grad_query, grad_key, grad_value = deliver(
        nz, nctx, rows_here, global_blocks, dqo, sums, rank
    )

    def dense_query(grad_query):
        return lax.all_to_all(dqo[:, :HD], "ctx", split_axis=0, concat_axis=1, tiled=True)

    grad_query = lax.cond(crowded, dense_query, lambda grad_query: grad_query, grad_query)
    return (context, grad_query, grad_key, grad_value)


def solution(mesh):
    split = P(("fsdp", "ctx"), None)
    return jax.shard_map(
        body,
        mesh=mesh,
        in_specs=(split, split, split, P("fsdp", None), split, P(), P(), P("fsdp", "ctx", None)),
        out_specs=(split, split, split, split),
        check_vma=False,
    )
```

```python
import functools
import math

import jax
import jax.numpy as jnp
from jax import lax
from jax.experimental import pallas as pl
from jax.experimental.pallas import tpu as pltpu
from jax.sharding import PartitionSpec as P

HD = 64
BLK = 64
GLOB = 2
SLOTS = 8


def contract(a, b, da, db):
    return lax.dot_general(a, b, (((da,), (db,)), ((), ())), preferred_element_type=jnp.float32)


def attend_kernel(glob_ref, pick_ref, kv_ref, qg_ref, dqo_ref, sum_ref, dkv_ref):
    width = 2 * HD
    scale = math.log2(math.e) / math.sqrt(HD)
    low = lax.broadcasted_iota(jnp.int32, (BLK, width), 1) < HD
    zero = jnp.zeros((BLK, width), jnp.bfloat16)
    dkv_ref[...] = jnp.zeros_like(dkv_ref)
    blocks = kv_ref.shape[0] // BLK
    local_blocks = qg_ref.shape[0] // BLK
    first_block = lax.axis_index("fsdp") * local_blocks
    last_block = local_blocks * lax.axis_size("fsdp") - 1
    lower = lax.broadcasted_iota(jnp.int32, (1, width), 1) < HD

    def candidates(i):
        current = first_block + i
        far = [glob_ref[g] for g in range(GLOB)] + [pick_ref[r, i] for r in range(SLOTS - 3 - GLOB)]
        usable = [current > 0, current >= 0, current < last_block]
        for n, block in enumerate(far):
            good = jnp.abs(block - current) > 1
            for earlier in far[:n]:
                good = jnp.logical_and(good, block != earlier)
            usable.append(good)
        ids = [i, i + 1, i + 2] + [blocks - GLOB + g for g in range(GLOB)]
        ids += [block - first_block + 1 for block in far[GLOB:]]
        return ids, [jnp.where(good, 0.0, -1e30) for good in usable]

    def rows(block):
        return pl.ds(pl.multiple_of(block * BLK, BLK), BLK)

    def step(j, carry):
        first = qg_ref[rows(2 * j), :]
        second = qg_ref[rows(2 * j + 1), :]
        mixed = jnp.concatenate(
            [
                jnp.concatenate([jnp.where(low, first, zero), zero], axis=1),
                jnp.concatenate([zero, jnp.where(low, second, zero)], axis=1),
                jnp.concatenate([jnp.where(low, zero, first), zero], axis=1),
                jnp.concatenate([zero, jnp.where(low, zero, second)], axis=1),
            ],
            axis=0,
        )
        left, left_bias = candidates(2 * j)
        right, right_bias = candidates(2 * j + 1)
        both = jnp.concatenate(
            [
                jnp.concatenate([kv_ref[rows(a), :], kv_ref[rows(b), :]], axis=1)
                for a, b in zip(left, right)
            ],
            axis=0,
        )
        products = contract(both, mixed, 1, 1)
        scores = []
        for s in range(SLOTS):
            part = products[s * BLK : (s + 1) * BLK, :width]
            scores.append(part * scale + jnp.where(lower, left_bias[s], right_bias[s]))
        highest = functools.reduce(jnp.maximum, scores)
        highest = jnp.max(highest, axis=0, keepdims=True)
        raised = [jnp.exp2(part - highest) for part in scores]
        total = jnp.sum(functools.reduce(jnp.add, raised), axis=0, keepdims=True)
        inverse = 1.0 / total
        probs = [part * inverse for part in raised]
        grads = [products[s * BLK : (s + 1) * BLK, width:] for s in range(SLOTS)]
        inner = functools.reduce(jnp.add, [p * g for p, g in zip(probs, grads)])
        inner = jnp.sum(inner, axis=0, keepdims=True)
        weights = jnp.concatenate(
            [
                jnp.concatenate(
                    [(p * (g - inner)).astype(jnp.bfloat16), p.astype(jnp.bfloat16)], axis=1
                )
                for p, g in zip(probs, grads)
            ],
            axis=0,
        )
        sums = contract(weights, both, 0, 0)
        eighth = jnp.where(low, 1.0 / math.sqrt(HD), 1.0)
        out_first = jnp.where(low, sums[:BLK, :width], sums[2 * BLK : 3 * BLK, :width]) * eighth
        out_second = jnp.where(low, sums[BLK : 2 * BLK, width:], sums[3 * BLK :, width:]) * eighth
        dqo_ref[rows(2 * j), :] = out_first.astype(jnp.bfloat16)
        dqo_ref[rows(2 * j + 1), :] = out_second.astype(jnp.bfloat16)
        terms = contract(weights, mixed, 1, 0)

        def term(s, side):
            return terms[s * BLK : (s + 1) * BLK, side * width : (side + 1) * width]

        dkv_ref[rows(2 * j), :] += term(0, 0)
        dkv_ref[rows(2 * j + 1), :] += term(1, 0) + term(0, 1)
        dkv_ref[rows(2 * j + 2), :] += term(2, 0) + term(1, 1)
        dkv_ref[rows(2 * j + 3), :] += term(2, 1)
        for s in range(3, 3 + GLOB):
            dkv_ref[rows(blocks - GLOB + s - 3), :] += term(s, 0) + term(s, 1)
        for s in range(3 + GLOB, SLOTS):
            dkv_ref[rows(left[s]), :] += term(s, 0)
            dkv_ref[rows(right[s]), :] += term(s, 1)
        return carry

    lax.fori_loop(0, local_blocks // 2, step, 0, unroll=2)
    eighth = jnp.where(low, 1.0 / math.sqrt(HD), 1.0)

    def finish(b, carry):
        sum_ref[rows(b), :] = (dkv_ref[rows(b), :] * eighth).astype(jnp.bfloat16)
        return carry

    lax.fori_loop(0, blocks, finish, 0, unroll=4)


def attend(global_blocks, picks, kv, qg):
    smem, vmem = pl.BlockSpec(memory_space=pltpu.SMEM), pl.BlockSpec(memory_space=pltpu.VMEM)
    return pl.pallas_call(
        attend_kernel,
        out_shape=(
            jax.ShapeDtypeStruct(qg.shape, jnp.bfloat16),
            jax.ShapeDtypeStruct(kv.shape, jnp.bfloat16),
        ),
        in_specs=[smem, smem, vmem, vmem],
        out_specs=(vmem, vmem),
        scratch_shapes=[pltpu.VMEM(kv.shape, jnp.float32)],
        compiler_params=pltpu.CompilerParams(vmem_limit_bytes=48 * 1024 * 1024),
        name="attend",
    )(global_blocks, picks, kv, qg)


CAP = 32
MESH = pl.DeviceIdType.MESH


def place(nz, nctx):
    z = lax.axis_index("fsdp")
    c = lax.axis_index("ctx")
    return z, c


def greet(nz, nctx):
    z, c = place(nz, nctx)
    barrier = pltpu.get_barrier_semaphore()

    def plane(d, carry):
        peer = lax.rem(c + d, nctx)
        pl.semaphore_signal(barrier, inc=1, device_id=(z, peer), device_id_type=MESH)
        return carry

    def column(d, carry):
        peer = lax.rem(z + d, nz)
        pl.semaphore_signal(barrier, inc=1, device_id=(peer, c), device_id_type=MESH)
        return carry

    lax.fori_loop(1, nctx, plane, 0)
    lax.fori_loop(1, nz, column, 0)


def meet(nz, nctx):
    pl.semaphore_wait(pltpu.get_barrier_semaphore(), nctx + nz - 2)


def plane_copy(nz, nctx, d, src, dst, send, recv):
    z, c = place(nz, nctx)
    peer = lax.rem(c + d, nctx)
    return pltpu.make_async_remote_copy(
        src_ref=src(peer),
        dst_ref=dst(c),
        send_sem=send,
        recv_sem=recv,
        device_id=(z, peer),
        device_id_type=MESH,
    )


def all_of(view, send, recv):
    z, c = lax.axis_index("fsdp"), lax.axis_index("ctx")
    return pltpu.make_async_remote_copy(
        src_ref=view,
        dst_ref=view,
        send_sem=send,
        recv_sem=recv,
        device_id=(z, lax.bitwise_xor(c, 1)),
        device_id_type=MESH,
    )


def column_copy(peer, src, dst, send, recv):
    c = lax.axis_index("ctx")
    return pltpu.make_async_remote_copy(
        src_ref=src,
        dst_ref=dst,
        send_sem=send,
        recv_sem=recv,
        device_id=(peer, c),
        device_id_type=MESH,
    )


def inner_copies(nz, nctx, side, src, buf, send, recv):
    z, c = place(nz, nctx)
    group, member = z // side, lax.rem(z, side)
    return [
        column_copy(
            group * side + lax.rem(member + e, side), src, buf.at[e], send.at[e], recv.at[e]
        )
        for e in range(1, side)
    ]


def outer_copies(nz, nctx, side, src, buf, send, recv):
    z, c = place(nz, nctx)
    group, member = z // side, lax.rem(z, side)
    groups = nz // side
    return [
        column_copy(
            lax.rem(group + e, groups) * side + member, src, buf.at[e], send.at[e], recv.at[e]
        )
        for e in range(1, groups)
    ]


def edge_copies(nz, down_src, down_dst, up_src, up_dst, send, recv):
    z = lax.axis_index("fsdp")
    down = column_copy(jnp.maximum(z - 1, 0), down_src, down_dst, send.at[0], recv.at[0])
    up = column_copy(jnp.minimum(z + 1, nz - 1), up_src, up_dst, send.at[1], recv.at[1])
    return down, up


def halves(x):
    return jnp.concatenate([x[:, HD:], x[:, :HD]], axis=1)


def chosen(rank_row):
    order = lax.broadcasted_iota(jnp.int32, (CAP, rank_row.shape[1]), 0).astype(jnp.float32)
    return jnp.where(order == rank_row, 1.0, 0.0).astype(jnp.bfloat16)


def square(n):
    return max(s for s in range(1, n + 1) if s * s <= n)


def collect_kernel(
    nz, nctx, glob_ref, q_ref, k_ref, v_ref, ct_ref, w_ref, pos_ref,
    kv_ref, qg_ref, rank_ref, most_ref,
    kv_pack, q_pack, q_all, up_own, up_all, w_all, p_out, p_in, g_all, count, g_own, g_in, g_mid, g_out,
    kv_send, kv_recv, q_send, q_recv, up_send, up_recv, w_send, w_recv, a_send, a_recv, p_send, p_recv,
    edge_send, edge_recv, in_send, in_recv, out_send, out_recv, pair_send, pair_recv, own_sem,
):
    z, c = place(nz, nctx)
    chip, core = c // 2, lax.rem(c, 2)
    cuts = square(nctx // 2)
    x, y = chip // cuts, lax.rem(chip, cuts)
    rows = q_ref.shape[0]
    wide = q_ref.shape[1]
    depth = wide // cuts
    side = square(nz)
    local_blocks = nctx * rows // BLK
    partner = 2 * chip + 1 - core
    low = lax.broadcasted_iota(jnp.int32, (BLK, 2 * HD), 1) < HD
    greet(nz, nctx)

    for t in range(nctx // 2):
        columns = slice(2 * t * HD, 2 * (t + 1) * HD)
        k_two, v_two = k_ref[:, columns], v_ref[:, columns]
        kv_pack[2 * t] = jnp.concatenate([k_two[:, :HD], v_two[:, :HD]], axis=1)
        kv_pack[2 * t + 1] = jnp.concatenate([k_two[:, HD:], v_two[:, HD:]], axis=1)
    meet(nz, nctx)

    def kv_copy(d):
        return plane_copy(
            nz, nctx, d, lambda p: kv_pack.at[p],
            lambda s: kv_ref.at[pl.ds(pl.multiple_of(BLK + s * rows, BLK), rows)], kv_send, kv_recv,
        )

    def kv_go(d, carry):
        kv_copy(d).start()
        return carry

    column_parts = max(1, depth // 256)
    piece_rows = rows * column_parts // nz

    def piece_at(i, begin):
        return (
            pl.ds(pl.multiple_of((i // column_parts) * piece_rows, piece_rows), piece_rows),
            pl.ds(
                pl.multiple_of(
                    begin + core * (depth // 2) + lax.rem(i, column_parts) * 128, 128
                ),
                128,
            ),
        )

    def weight_out(d):
        i = lax.rem(z + d, nz)
        return column_copy(
            i, w_ref.at[piece_at(i, x * depth)], w_all.at[(z // cuts,) + piece_at(i, 0)],
            w_send.at[d], w_recv.at[z // cuts],
        )

    own_piece = pltpu.make_async_copy(
        w_ref.at[piece_at(z, x * depth)], w_all.at[(z // cuts,) + piece_at(z, 0)], own_sem
    )
    is_source = lax.rem(z, cuts) == y

    @pl.when(is_source)
    def _():
        def go(d, carry):
            weight_out(d).start()
            return carry

        lax.fori_loop(1, nz, go, 0)
        own_piece.start()

    lax.fori_loop(1, nctx, kv_go, 0)
    kv_ref[pl.ds(pl.multiple_of(BLK + c * rows, BLK), rows)] = kv_pack[c]

    for t in range(nctx // 2):
        columns = slice(2 * t * HD, 2 * (t + 1) * HD)
        top, bottom = q_ref[:BLK, columns], q_ref[BLK:, columns]
        q_pack[2 * t] = jnp.concatenate([top[:, :HD], bottom[:, :HD]], axis=1)
        q_pack[2 * t + 1] = jnp.concatenate([top[:, HD:], bottom[:, HD:]], axis=1)

    for s in range(cuts):

        @pl.when(z != s * cuts + y)
        def _():
            column_copy(
                lax.rem(z + 1, nz), w_ref.at[piece_at(z, x * depth)], w_all.at[(s,) + piece_at(z, 0)],
                w_send.at[0], w_recv.at[s],
            ).wait_recv()

    @pl.when(is_source)
    def _():
        own_piece.wait()

    def weight_copy(d, incoming=False):
        at = w_all.at[
            (slice(None),) + piece_at(lax.rem(z - d + nz, nz) if incoming else z, 0)
        ]
        return column_copy(lax.rem(z + d, nz), at, at, a_send.at[d], a_recv.at[d])

    def weight_go(d, carry):
        weight_copy(d).start()
        return carry

    lax.fori_loop(1, nz, weight_go, 0)

    devices = nz * nctx
    count[...] = jnp.zeros_like(count)
    span = 2 * pos_ref.shape[1]
    group_ids = lax.broadcasted_iota(jnp.int32, (devices, span), 0)
    inside_ids = lax.broadcasted_iota(jnp.int32, (rows, span), 0)

    def tally(i, carry):
        pos = jnp.concatenate([pos_ref[pl.ds(2 * i, 1), :], pos_ref[pl.ds(2 * i + 1, 1), :]], axis=1)
        group = pos // rows
        inside = pos - group * rows
        hit = jnp.where(group_ids == group, 1.0, 0.0).astype(jnp.bfloat16)
        spot = jnp.where(inside_ids == inside, 1.0, 0.0).astype(jnp.bfloat16)
        count[...] += contract(hit, spot, 1, 1)
        return carry

    lax.fori_loop(0, pos_ref.shape[0] // 2, tally, 0)
    masked = jnp.where(count[...] > 0.5, 1.0, 0.0)
    before = lax.broadcasted_iota(jnp.int32, (rows, rows), 0) < lax.broadcasted_iota(
        jnp.int32, (rows, rows), 1
    )
    rank = contract(masked.astype(jnp.bfloat16), jnp.where(before, 1.0, 0.0).astype(jnp.bfloat16), 1, 0)
    count[...] = jnp.where(masked > 0.5, rank, -1.0)
    most = jnp.max(jnp.max(count[...], axis=0, keepdims=True), axis=1, keepdims=True)
    most_ref[...] = jnp.broadcast_to(most, most_ref.shape)
    rank_ref[...] = count[pl.ds(pl.multiple_of(z * nctx, nctx), nctx), :]
    mine = chosen(rank_ref[pl.ds(c, 1), :])
    up_own[...] = contract(mine, ct_ref[...], 1, 0).astype(jnp.bfloat16)

    def share(i):
        return pl.ds(pl.multiple_of(i * depth, depth), depth)

    def up_copy(d):
        target = lax.rem(chip + d, nctx // 2)
        return pltpu.make_async_remote_copy(
            src_ref=up_own.at[:, share(target // cuts)],
            dst_ref=up_all.at[pl.ds(pl.multiple_of(chip * CAP, CAP), CAP)],
            send_sem=up_send,
            recv_sem=up_recv,
            device_id=(z, 2 * target + core),
            device_id_type=MESH,
        )

    def up_go(d, carry):
        up_copy(d).start()
        return carry

    lax.fori_loop(1, nctx // 2, up_go, 0)
    up_all[pl.ds(pl.multiple_of(chip * CAP, CAP), CAP)] = up_own[:, share(x)]

    def q_go(d, carry):
        plane_copy(
            nz, nctx, d, lambda p: q_pack.at[p], lambda s: q_all.at[s], q_send, q_recv
        ).start()
        return carry

    lax.fori_loop(1, nctx, q_go, 0)
    q_all[c] = q_pack[c]

    all_of(kv_ref.at[pl.ds(0, (nctx - 1) * rows)], kv_send, kv_recv).wait_recv()
    low_edge = kv_ref.at[pl.ds(0, BLK)]
    high_edge = kv_ref.at[pl.ds((local_blocks + 1) * BLK, BLK)]
    down, up = edge_copies(
        nz, kv_ref.at[pl.ds(BLK, BLK)], high_edge, kv_ref.at[pl.ds(local_blocks * BLK, BLK)],
        low_edge, edge_send, edge_recv,
    )
    wanted = [glob_ref[i] - z * local_blocks for i in range(GLOB)]

    def pick(b, totals):
        block = kv_ref[pl.ds(pl.multiple_of(BLK + b * BLK, BLK), BLK), :]
        return tuple(
            jnp.where(jnp.full(block.shape, wanted[i] == b), block, totals[i]) for i in range(GLOB)
        )

    nothing = jnp.zeros((BLK, 2 * HD), jnp.bfloat16)
    picked = lax.fori_loop(0, local_blocks, pick, (nothing,) * GLOB, unroll=8)
    g_own[...] = jnp.concatenate(picked, axis=0)
    stage_in = inner_copies(nz, nctx, side, g_own, g_in, in_send, in_recv)
    for copy in stage_in:
        copy.start()

    @pl.when(z > 0)
    def _():
        down.start()

    @pl.when(z < nz - 1)
    def _():
        up.start()

    half = pl.ds(pl.multiple_of(core * (depth // 2), depth // 2), depth // 2)
    other_half = pl.ds(pl.multiple_of((1 - core) * (depth // 2), depth // 2), depth // 2)

    def pair_copy(src, dst, i):
        return pltpu.make_async_remote_copy(
            src_ref=src,
            dst_ref=dst,
            send_sem=pair_send.at[i],
            recv_sem=pair_recv.at[i],
            device_id=(z, partner),
            device_id_type=MESH,
        )

    cross_out = pair_copy(w_all.at[:, :, half], w_all.at[:, :, half], 0)
    cross_in = pair_copy(w_all.at[:, :, other_half], w_all.at[:, :, other_half], 0)

    def weight_in(d, carry):
        weight_copy(d, True).wait_recv()
        return carry

    lax.fori_loop(1, nz, weight_in, 0)
    cross_out.start()

    total = g_own[...].astype(jnp.float32)
    for e, copy in enumerate(stage_in):
        copy.wait_recv()
        total = total + g_in[e + 1].astype(jnp.float32)
    g_mid[...] = total.astype(jnp.bfloat16)
    stage_out = outer_copies(nz, nctx, side, g_mid, g_out, out_send, out_recv)
    for copy in stage_out:
        copy.start()

    all_of(up_all.at[pl.ds(0, (nctx // 2 - 1) * CAP)], up_send, up_recv).wait_recv()
    cross_in.wait_recv()
    for s in range(cuts):
        p_out[s] = contract(up_all[...], w_all[s], 1, 1)

    def partial_copy(e):
        target = lax.rem(x + e, cuts)
        return pltpu.make_async_remote_copy(
            src_ref=p_out.at[target],
            dst_ref=p_in.at[e],
            send_sem=p_send.at[e],
            recv_sem=p_recv.at[e],
            device_id=(z, 2 * (target * cuts + y) + core),
            device_id_type=MESH,
        )

    partials = [partial_copy(e) for e in range(1, cuts)]
    for copy in partials:
        copy.start()

    @pl.when(z > 0)
    def _():
        column_copy(jnp.maximum(z - 1, 0), low_edge, low_edge, edge_send.at[1], edge_recv.at[1]).wait_recv()

    @pl.when(z == 0)
    def _():
        kv_ref[pl.ds(0, BLK), :] = nothing

    @pl.when(z < nz - 1)
    def _():
        column_copy(
            jnp.minimum(z + 1, nz - 1), high_edge, high_edge, edge_send.at[0], edge_recv.at[0]
        ).wait_recv()

    @pl.when(z == nz - 1)
    def _():
        kv_ref[pl.ds((local_blocks + 1) * BLK, BLK), :] = nothing

    total = g_mid[...].astype(jnp.float32)
    for e, copy in enumerate(stage_out):
        copy.wait_recv()
        total = total + g_out[e + 1].astype(jnp.float32)
    kv_ref[pl.ds((local_blocks + 2) * BLK, GLOB * BLK), :] = total.astype(jnp.bfloat16)

    grad = p_out[x]
    for e, copy in enumerate(partials):
        copy.wait_recv()
        grad = grad + p_in[e + 1]
    g_all[core] = grad.astype(jnp.bfloat16)
    swap_out = pair_copy(g_all.at[core], g_all.at[core], 1)
    swap_in = pair_copy(g_all.at[1 - core], g_all.at[1 - core], 1)
    swap_out.start()
    all_of(q_all.at[pl.ds(0, nctx - 1)], q_send, q_recv).wait_recv()
    swap_in.wait_recv()

    def expand(j, carry):
        marks = chosen(rank_ref[pl.ds(j, 1), :])
        compact = g_all[lax.rem(j, 2), pl.ds(pl.multiple_of((j // 2) * CAP, CAP), CAP), :]
        dense = contract(marks, compact, 0, 0).astype(jnp.bfloat16)
        dense = jnp.where(jnp.full(dense.shape, core == 0), halves(dense), dense)
        two = q_all[j]
        begin = pl.multiple_of(j * rows, rows)
        qg_ref[pl.ds(begin, BLK), :] = jnp.where(low, two, dense[:BLK])
        qg_ref[pl.ds(begin + BLK, BLK), :] = jnp.where(low, halves(two), dense[BLK:])
        return carry

    lax.fori_loop(0, nctx, expand, 0, unroll=4)

    all_of(kv_pack.at[pl.ds(0, nctx - 1)], kv_send, kv_recv).wait_send()
    all_of(q_pack.at[pl.ds(0, nctx - 1)], q_send, q_recv).wait_send()
    all_of(up_all.at[pl.ds(0, (nctx // 2 - 1) * CAP)], up_send, up_recv).wait_send()

    def left_weight(d, carry):
        weight_copy(d).wait_send()

        @pl.when(is_source)
        def _():
            weight_out(d).wait_send()

        return carry

    lax.fori_loop(1, nz, left_weight, 0)

    @pl.when(z > 0)
    def _():
        down.wait_send()

    @pl.when(z < nz - 1)
    def _():
        up.wait_send()

    for copy in stage_in + stage_out + partials:
        copy.wait_send()
    cross_out.wait_send()
    swap_out.wait_send()


def collect(nz, nctx, global_blocks, q, k, v, ct, w, positions):
    rows, wide = q.shape
    region = nctx * rows
    side, cuts = square(nz), square(nctx // 2)
    half = jnp.bfloat16
    dma = pltpu.SemaphoreType.DMA
    vmem = pl.BlockSpec(memory_space=pltpu.VMEM)
    return pl.pallas_call(
        functools.partial(collect_kernel, nz, nctx),
        out_shape=(
            jax.ShapeDtypeStruct((region + (2 + GLOB) * BLK, 2 * HD), half),
            jax.ShapeDtypeStruct((region, 2 * HD), half),
            jax.ShapeDtypeStruct((nctx, rows), jnp.float32),
            jax.ShapeDtypeStruct((8, 128), jnp.float32),
        ),
        in_specs=[pl.BlockSpec(memory_space=pltpu.SMEM)] + [vmem] * 6,
        out_specs=(vmem,) * 4,
        scratch_shapes=[
            pltpu.VMEM((nctx, rows, 2 * HD), half),
            pltpu.VMEM((nctx, BLK, 2 * HD), half),
            pltpu.VMEM((nctx, BLK, 2 * HD), half),
            pltpu.VMEM((CAP, wide), half),
            pltpu.VMEM((nctx // 2 * CAP, wide // cuts), half),
            pltpu.VMEM((cuts, rows, wide // cuts), half),
            pltpu.VMEM((cuts, nctx // 2 * CAP, 2 * HD), jnp.float32),
            pltpu.VMEM((cuts, nctx // 2 * CAP, 2 * HD), jnp.float32),
            pltpu.VMEM((2, nctx // 2 * CAP, 2 * HD), half),
            pltpu.VMEM((nz * nctx, rows), jnp.float32),
            pltpu.VMEM((GLOB * BLK, 2 * HD), half),
            pltpu.VMEM((side, GLOB * BLK, 2 * HD), half),
            pltpu.VMEM((GLOB * BLK, 2 * HD), half),
            pltpu.VMEM((nz // side, GLOB * BLK, 2 * HD), half),
            dma(()), dma(()), dma(()), dma(()), dma(()), dma(()),
            dma((nz,)), dma((cuts,)), dma((nz,)), dma((nz,)), dma((cuts,)), dma((cuts,)),
            dma((2,)), dma((2,)),
            dma((side,)), dma((side,)), dma((nz // side,)), dma((nz // side,)),
            dma((2,)), dma((2,)), dma(()),
        ],
        compiler_params=pltpu.CompilerParams(
            collective_id=0, has_side_effects=True, vmem_limit_bytes=56 * 1024 * 1024
        ),
        name="collect",
    )(global_blocks, q, k, v, ct, w, positions.reshape(-1, 128))


def deliver_kernel(
    nz, nctx, glob_ref, dqo_ref, sums_ref, rank_ref,
    oq_all, kv_all,
    oq_pack, kv_pack, edge_out, edge_in, g_own, g_in, g_mid, g_out,
    oq_send, oq_recv, kv_send, kv_recv, edge_send, edge_recv, in_send, in_recv, out_send, out_recv,
):
    z, c = place(nz, nctx)
    rows = kv_all.shape[1]
    side = square(nz)
    local_blocks = nctx * rows // BLK
    few = CAP // 2
    high_begin = (local_blocks + 1) * BLK
    greet(nz, nctx)
    edge_out[0] = sums_ref[pl.ds(0, BLK), :]
    edge_out[1] = sums_ref[pl.ds(high_begin, BLK), :]
    g_own[...] = sums_ref[pl.ds(high_begin + BLK, GLOB * BLK), :]

    def shrink(j, carry):
        both = dqo_ref[pl.ds(pl.multiple_of(j * rows, rows), rows), :]
        oq_pack[j, pl.ds(0, BLK), :] = jnp.concatenate([both[:BLK, HD:], both[BLK:, HD:]], axis=1)
        picked = contract(chosen(rank_ref[pl.ds(j, 1), :]), both, 1, 0).astype(jnp.bfloat16)
        oq_pack[j, pl.ds(BLK, few), :] = jnp.concatenate([picked[:few, :HD], picked[few:, :HD]], axis=1)
        return carry

    lax.fori_loop(0, nctx, shrink, 0, unroll=4)
    meet(nz, nctx)
    stage_in = inner_copies(nz, nctx, side, g_own, g_in, in_send, in_recv)
    for copy in stage_in:
        copy.start()
    down, up = edge_copies(
        nz, edge_out.at[0], edge_in.at[0], edge_out.at[1], edge_in.at[1], edge_send, edge_recv
    )

    @pl.when(z > 0)
    def _():
        down.start()

    @pl.when(z < nz - 1)
    def _():
        up.start()

    def oq_go(d, carry):
        plane_copy(
            nz, nctx, d, lambda p: oq_pack.at[p], lambda s: oq_all.at[s], oq_send, oq_recv
        ).start()
        return carry

    lax.fori_loop(1, nctx, oq_go, 0)
    oq_all[c] = oq_pack[c]

    total = g_own[...].astype(jnp.float32)
    for e, copy in enumerate(stage_in):
        copy.wait_recv()
        total = total + g_in[e + 1].astype(jnp.float32)
    g_mid[...] = total.astype(jnp.bfloat16)
    stage_out = outer_copies(nz, nctx, side, g_mid, g_out, out_send, out_recv)
    for copy in stage_out:
        copy.start()

    @pl.when(z > 0)
    def _():
        column_copy(
            jnp.maximum(z - 1, 0), edge_out.at[1], edge_in.at[1], edge_send.at[1], edge_recv.at[1]
        ).wait_recv()

    @pl.when(z == 0)
    def _():
        edge_in[1] = jnp.zeros_like(edge_in[1])

    @pl.when(z < nz - 1)
    def _():
        column_copy(
            jnp.minimum(z + 1, nz - 1), edge_out.at[0], edge_in.at[0], edge_send.at[0], edge_recv.at[0]
        ).wait_recv()

    @pl.when(z == nz - 1)
    def _():
        edge_in[0] = jnp.zeros_like(edge_in[0])

    for copy in stage_out:
        copy.wait_recv()
    for e in range(1, nz // side):
        total = total + g_out[e].astype(jnp.float32)
    wanted = [glob_ref[i] - z * local_blocks for i in range(GLOB)]

    def settle(j, carry):
        for side_of in range(2):
            b = 2 * j + side_of
            term = sums_ref[pl.ds(pl.multiple_of((b + 1) * BLK, BLK), BLK), :].astype(jnp.float32)
            for i in range(GLOB):
                extra = total[i * BLK : (i + 1) * BLK]
                term = term + jnp.where(jnp.full(extra.shape, wanted[i] == b), extra, 0.0)
            edge = edge_in[1 - side_of].astype(jnp.float32)
            at_edge = j == (nctx - 1) * side_of
            term = term + jnp.where(jnp.full(edge.shape, at_edge), edge, 0.0)
            kv_pack[j, pl.ds(side_of * BLK, BLK), :] = term.astype(jnp.bfloat16)
        return carry

    lax.fori_loop(0, nctx, settle, 0, unroll=2)

    def kv_go(d, carry):
        plane_copy(
            nz, nctx, d, lambda p: kv_pack.at[p], lambda s: kv_all.at[s], kv_send, kv_recv
        ).start()
        return carry

    lax.fori_loop(1, nctx, kv_go, 0)
    kv_all[c] = kv_pack[c]

    all_of(oq_all.at[pl.ds(0, nctx - 1)], oq_send, oq_recv).wait_recv()
    all_of(kv_all.at[pl.ds(0, nctx - 1)], kv_send, kv_recv).wait_recv()
    all_of(oq_pack.at[pl.ds(0, nctx - 1)], oq_send, oq_recv).wait_send()
    all_of(kv_pack.at[pl.ds(0, nctx - 1)], kv_send, kv_recv).wait_send()

    @pl.when(z > 0)
    def _():
        down.wait_send()

    @pl.when(z < nz - 1)
    def _():
        up.wait_send()

    for copy in stage_in + stage_out:
        copy.wait_send()


def deliver(nz, nctx, rows, global_blocks, dqo, sums, rank):
    side = square(nz)
    half = jnp.bfloat16
    dma = pltpu.SemaphoreType.DMA
    vmem = pl.BlockSpec(memory_space=pltpu.VMEM)
    return pl.pallas_call(
        functools.partial(deliver_kernel, nz, nctx),
        out_shape=(
            jax.ShapeDtypeStruct((nctx, BLK + CAP // 2, 2 * HD), half),
            jax.ShapeDtypeStruct((nctx, rows, 2 * HD), half),
        ),
        in_specs=[pl.BlockSpec(memory_space=pltpu.SMEM)] + [vmem] * 3,
        out_specs=(vmem,) * 2,
        scratch_shapes=[
            pltpu.VMEM((nctx, BLK + CAP // 2, 2 * HD), half),
            pltpu.VMEM((nctx, rows, 2 * HD), half),
            pltpu.VMEM((2, BLK, 2 * HD), half),
            pltpu.VMEM((2, BLK, 2 * HD), half),
            pltpu.VMEM((GLOB * BLK, 2 * HD), half),
            pltpu.VMEM((side, GLOB * BLK, 2 * HD), half),
            pltpu.VMEM((GLOB * BLK, 2 * HD), half),
            pltpu.VMEM((nz // side, GLOB * BLK, 2 * HD), half),
            dma(()), dma(()), dma(()), dma(()),
            dma((2,)), dma((2,)),
            dma((side,)), dma((side,)), dma((nz // side,)), dma((nz // side,)),
        ],
        compiler_params=pltpu.CompilerParams(
            collective_id=1, has_side_effects=True, vmem_limit_bytes=56 * 1024 * 1024
        ),
        name="deliver",
    )(global_blocks, dqo, sums, rank)


def spread_kernel(oq_ref, kv_ref, rank_ref, most_ref, full_ref, o_ref, dq_ref, dk_ref, dv_ref, compact):
    few = CAP // 2
    for t in range(oq_ref.shape[0] // 2):
        columns = slice(2 * t * HD, 2 * (t + 1) * HD)
        first, second = oq_ref[2 * t], oq_ref[2 * t + 1]
        o_ref[:BLK, columns] = jnp.concatenate([first[:BLK, :HD], second[:BLK, :HD]], axis=1)
        o_ref[BLK:, columns] = jnp.concatenate([first[:BLK, HD:], second[:BLK, HD:]], axis=1)
        compact[:few, columns] = jnp.concatenate([first[BLK:, :HD], second[BLK:, :HD]], axis=1)
        compact[few:, columns] = jnp.concatenate([first[BLK:, HD:], second[BLK:, HD:]], axis=1)
        first, second = kv_ref[2 * t], kv_ref[2 * t + 1]
        dk_ref[:, columns] = jnp.concatenate([first[:, :HD], second[:, :HD]], axis=1)
        dv_ref[:, columns] = jnp.concatenate([first[:, HD:], second[:, HD:]], axis=1)
    marks = chosen(rank_ref[pl.ds(lax.axis_index("ctx"), 1), :])
    spread = contract(marks, compact[...], 0, 0).astype(jnp.bfloat16)
    crowded = jnp.broadcast_to(most_ref[:1, :1], spread.shape) > CAP - 0.5
    dq_ref[...] = jnp.where(crowded, full_ref[...], spread)


def spread(oq, kv, rank, most, full):
    vmem = pl.BlockSpec(memory_space=pltpu.VMEM)
    return pl.pallas_call(
        spread_kernel,
        out_shape=(jax.ShapeDtypeStruct(full.shape, full.dtype),) * 4,
        in_specs=[vmem] * 5,
        out_specs=(vmem,) * 4,
        scratch_shapes=[pltpu.VMEM((CAP, full.shape[1]), full.dtype)],
        compiler_params=pltpu.CompilerParams(vmem_limit_bytes=48 * 1024 * 1024),
        name="spread",
    )(oq, kv, rank, most, full)


def body(queries, keys, values, out_weight, cotangent, positions, global_blocks, random_blocks):
    rows_here = queries.shape[0]
    nz, nctx = lax.axis_size("fsdp"), lax.axis_size("ctx")
    local_blocks = nctx * rows_here // BLK
    kv, qg, rank, most = collect(
        nz, nctx, global_blocks, queries, keys, values, cotangent, out_weight, positions
    )
    crowded = most[0, 0] > CAP - 0.5

    def dense_gradient(qg):
        offset = (lax.axis_index("fsdp") * nctx + lax.axis_index("ctx")) * rows_here
        places = offset + jnp.arange(rows_here, dtype=jnp.int32)
        masked = jnp.any(positions[:, None] == places[None, :], axis=0)
        upstream = jnp.where(masked[:, None], cotangent, jnp.zeros_like(cotangent))
        weight = lax.all_gather(out_weight, "fsdp", axis=0, tiled=True)
        grad = contract(upstream, weight, 1, 1).astype(jnp.bfloat16)
        grad = lax.all_to_all(grad, "ctx", split_axis=1, concat_axis=0, tiled=True)
        return jnp.concatenate([qg[:, :HD], grad], axis=1)

    qg = lax.cond(crowded, dense_gradient, lambda qg: qg, qg)
    picks = random_blocks.transpose(2, 1, 0).reshape(random_blocks.shape[2], local_blocks)
    dqo, sums = attend(global_blocks, picks, kv, qg)
    parts, key_values = deliver(nz, nctx, rows_here, global_blocks, dqo, sums, rank)

    def dense_query():
        return lax.all_to_all(dqo[:, :HD], "ctx", split_axis=0, concat_axis=1, tiled=True)

    full = lax.cond(crowded, dense_query, lambda: jnp.zeros_like(queries))
    return spread(parts, key_values, rank, most, full)


def solution(mesh):
    split = P(("fsdp", "ctx"), None)
    return jax.shard_map(
        body,
        mesh=mesh,
        in_specs=(split, split, split, P("fsdp", None), split, P(), P(), P("fsdp", "ctx", None)),
        out_specs=(split, split, split, split),
        check_vma=False,
    )
```

```python
import functools
import math

import jax
import jax.numpy as jnp
from jax import lax
from jax.experimental import pallas as pl
from jax.experimental.pallas import tpu as pltpu
from jax.sharding import PartitionSpec as P

HD = 64
BLK = 64
GLOB = 2
SLOTS = 8


def contract(a, b, da, db):
    return lax.dot_general(a, b, (((da,), (db,)), ((), ())), preferred_element_type=jnp.float32)


def attend_kernel(glob_ref, pick_ref, kv_ref, qg_ref, dqo_ref, sum_ref, dkv_ref):
    width = 2 * HD
    scale = math.log2(math.e) / math.sqrt(HD)
    low = lax.broadcasted_iota(jnp.int32, (BLK, width), 1) < HD
    zero = jnp.zeros((BLK, width), jnp.bfloat16)
    dkv_ref[...] = jnp.zeros_like(dkv_ref)
    blocks = kv_ref.shape[0] // BLK
    local_blocks = qg_ref.shape[0] // BLK
    first_block = lax.axis_index("fsdp") * local_blocks
    last_block = local_blocks * lax.axis_size("fsdp") - 1
    lower = lax.broadcasted_iota(jnp.int32, (1, width), 1) < HD

    def candidates(i):
        current = first_block + i
        far = [glob_ref[g] for g in range(GLOB)] + [pick_ref[r, i] for r in range(SLOTS - 3 - GLOB)]
        usable = [current > 0, current >= 0, current < last_block]
        for n, block in enumerate(far):
            good = jnp.abs(block - current) > 1
            for earlier in far[:n]:
                good = jnp.logical_and(good, block != earlier)
            usable.append(good)
        ids = [i, i + 1, i + 2] + [blocks - GLOB + g for g in range(GLOB)]
        ids += [block - first_block + 1 for block in far[GLOB:]]
        return ids, [jnp.where(good, 0.0, -1e30) for good in usable]

    def rows(block):
        return pl.ds(pl.multiple_of(block * BLK, BLK), BLK)

    def step(j, carry):
        first = qg_ref[rows(2 * j), :]
        second = qg_ref[rows(2 * j + 1), :]
        mixed = jnp.concatenate(
            [
                jnp.concatenate([jnp.where(low, first, zero), zero], axis=1),
                jnp.concatenate([zero, jnp.where(low, second, zero)], axis=1),
                jnp.concatenate([jnp.where(low, zero, first), zero], axis=1),
                jnp.concatenate([zero, jnp.where(low, zero, second)], axis=1),
            ],
            axis=0,
        )
        left, left_bias = candidates(2 * j)
        right, right_bias = candidates(2 * j + 1)
        both = jnp.concatenate(
            [
                jnp.concatenate([kv_ref[rows(a), :], kv_ref[rows(b), :]], axis=1)
                for a, b in zip(left, right)
            ],
            axis=0,
        )
        products = contract(both, mixed, 1, 1)
        scores = []
        for s in range(SLOTS):
            part = products[s * BLK : (s + 1) * BLK, :width]
            scores.append(part * scale + jnp.where(lower, left_bias[s], right_bias[s]))
        highest = functools.reduce(jnp.maximum, scores)
        highest = jnp.max(highest, axis=0, keepdims=True)
        raised = [jnp.exp2(part - highest) for part in scores]
        total = jnp.sum(functools.reduce(jnp.add, raised), axis=0, keepdims=True)
        inverse = 1.0 / total
        probs = [part * inverse for part in raised]
        grads = [products[s * BLK : (s + 1) * BLK, width:] for s in range(SLOTS)]
        inner = functools.reduce(jnp.add, [p * g for p, g in zip(probs, grads)])
        inner = jnp.sum(inner, axis=0, keepdims=True)
        weights = jnp.concatenate(
            [
                jnp.concatenate(
                    [(p * (g - inner)).astype(jnp.bfloat16), p.astype(jnp.bfloat16)], axis=1
                )
                for p, g in zip(probs, grads)
            ],
            axis=0,
        )
        sums = contract(weights, both, 0, 0)
        eighth = jnp.where(low, 1.0 / math.sqrt(HD), 1.0)
        out_first = jnp.where(low, sums[:BLK, :width], sums[2 * BLK : 3 * BLK, :width]) * eighth
        out_second = jnp.where(low, sums[BLK : 2 * BLK, width:], sums[3 * BLK :, width:]) * eighth
        dqo_ref[rows(2 * j), :] = out_first.astype(jnp.bfloat16)
        dqo_ref[rows(2 * j + 1), :] = out_second.astype(jnp.bfloat16)
        terms = contract(weights, mixed, 1, 0)

        def term(s, side):
            return terms[s * BLK : (s + 1) * BLK, side * width : (side + 1) * width]

        dkv_ref[rows(2 * j), :] += term(0, 0)
        dkv_ref[rows(2 * j + 1), :] += term(1, 0) + term(0, 1)
        dkv_ref[rows(2 * j + 2), :] += term(2, 0) + term(1, 1)
        dkv_ref[rows(2 * j + 3), :] += term(2, 1)
        for s in range(3, 3 + GLOB):
            dkv_ref[rows(blocks - GLOB + s - 3), :] += term(s, 0) + term(s, 1)
        for s in range(3 + GLOB, SLOTS):
            dkv_ref[rows(left[s]), :] += term(s, 0)
            dkv_ref[rows(right[s]), :] += term(s, 1)
        return carry

    lax.fori_loop(0, local_blocks // 2, step, 0, unroll=2)
    eighth = jnp.where(low, 1.0 / math.sqrt(HD), 1.0)

    def finish(b, carry):
        sum_ref[rows(b), :] = (dkv_ref[rows(b), :] * eighth).astype(jnp.bfloat16)
        return carry

    lax.fori_loop(0, blocks, finish, 0, unroll=4)


def attend(global_blocks, picks, kv, qg):
    smem, vmem = pl.BlockSpec(memory_space=pltpu.SMEM), pl.BlockSpec(memory_space=pltpu.VMEM)
    return pl.pallas_call(
        attend_kernel,
        out_shape=(
            jax.ShapeDtypeStruct(qg.shape, jnp.bfloat16),
            jax.ShapeDtypeStruct(kv.shape, jnp.bfloat16),
        ),
        in_specs=[smem, smem, vmem, vmem],
        out_specs=(vmem, vmem),
        scratch_shapes=[pltpu.VMEM(kv.shape, jnp.float32)],
        compiler_params=pltpu.CompilerParams(vmem_limit_bytes=48 * 1024 * 1024),
        name="attend",
    )(global_blocks, picks, kv, qg)


CAP = 32
MESH = pl.DeviceIdType.MESH


def place(nz, nctx):
    z = lax.axis_index("fsdp")
    c = lax.axis_index("ctx")
    return z, c


def greet(nz, nctx):
    z, c = place(nz, nctx)
    barrier = pltpu.get_barrier_semaphore()

    def plane(d, carry):
        peer = lax.rem(c + d, nctx)
        pl.semaphore_signal(barrier, inc=1, device_id=(z, peer), device_id_type=MESH)
        return carry

    def column(d, carry):
        peer = lax.rem(z + d, nz)
        pl.semaphore_signal(barrier, inc=1, device_id=(peer, c), device_id_type=MESH)
        return carry

    lax.fori_loop(1, nctx, plane, 0)
    lax.fori_loop(1, nz, column, 0)


def meet(nz, nctx):
    pl.semaphore_wait(pltpu.get_barrier_semaphore(), nctx + nz - 2)


def plane_copy(nz, nctx, d, src, dst, send, recv):
    z, c = place(nz, nctx)
    peer = lax.rem(c + d, nctx)
    return pltpu.make_async_remote_copy(
        src_ref=src(peer),
        dst_ref=dst(c),
        send_sem=send,
        recv_sem=recv,
        device_id=(z, peer),
        device_id_type=MESH,
    )


def all_of(view, send, recv):
    z, c = lax.axis_index("fsdp"), lax.axis_index("ctx")
    return pltpu.make_async_remote_copy(
        src_ref=view,
        dst_ref=view,
        send_sem=send,
        recv_sem=recv,
        device_id=(z, lax.bitwise_xor(c, 1)),
        device_id_type=MESH,
    )


def column_copy(peer, src, dst, send, recv):
    c = lax.axis_index("ctx")
    return pltpu.make_async_remote_copy(
        src_ref=src,
        dst_ref=dst,
        send_sem=send,
        recv_sem=recv,
        device_id=(peer, c),
        device_id_type=MESH,
    )


def inner_copies(nz, nctx, side, src, buf, send, recv):
    z, c = place(nz, nctx)
    group, member = z // side, lax.rem(z, side)
    return [
        column_copy(
            group * side + lax.rem(member + e, side), src, buf.at[e], send.at[e], recv.at[e]
        )
        for e in range(1, side)
    ]


def outer_copies(nz, nctx, side, src, buf, send, recv):
    z, c = place(nz, nctx)
    group, member = z // side, lax.rem(z, side)
    groups = nz // side
    return [
        column_copy(
            lax.rem(group + e, groups) * side + member, src, buf.at[e], send.at[e], recv.at[e]
        )
        for e in range(1, groups)
    ]


def edge_copies(nz, down_src, down_dst, up_src, up_dst, send, recv):
    z = lax.axis_index("fsdp")
    down = column_copy(jnp.maximum(z - 1, 0), down_src, down_dst, send.at[0], recv.at[0])
    up = column_copy(jnp.minimum(z + 1, nz - 1), up_src, up_dst, send.at[1], recv.at[1])
    return down, up


def halves(x):
    return jnp.concatenate([x[:, HD:], x[:, :HD]], axis=1)


def chosen(rank_row):
    order = lax.broadcasted_iota(jnp.int32, (CAP, rank_row.shape[1]), 0).astype(jnp.float32)
    return jnp.where(order == rank_row, 1.0, 0.0).astype(jnp.bfloat16)


def square(n):
    return max(s for s in range(1, n + 1) if s * s <= n)


def collect_kernel(
    nz, nctx, glob_ref, q_far, k_far, v_far, ct_far, w_ref, pos_ref,
    kv_ref, qg_ref, rank_ref, most_ref,
    kv_pack, q_pack, q_all, up_own, up_all, w_all, p_out, p_in, g_all, count, g_own, g_in, g_mid, g_out,
    kv_send, kv_recv, q_send, q_recv, up_send, up_recv, w_send, w_recv, a_send, a_recv, p_send, p_recv,
    edge_send, edge_recv, in_send, in_recv, out_send, out_recv, pair_send, pair_recv, own_sem,
    q_ref, k_ref, v_ref, ct_ref, load_sem,
):
    z, c = place(nz, nctx)
    chip, core = c // 2, lax.rem(c, 2)
    cuts = square(nctx // 2)
    x, y = chip // cuts, lax.rem(chip, cuts)
    loads = [
        pltpu.make_async_copy(far, near, load_sem.at[i])
        for i, (far, near) in enumerate(
            [(k_far, k_ref), (v_far, v_ref), (q_far, q_ref), (ct_far, ct_ref)]
        )
    ]
    for load in loads:
        load.start()
    rows = q_ref.shape[0]
    wide = q_ref.shape[1]
    depth = wide // cuts
    side = square(nz)
    local_blocks = nctx * rows // BLK
    partner = 2 * chip + 1 - core
    low = lax.broadcasted_iota(jnp.int32, (BLK, 2 * HD), 1) < HD
    greet(nz, nctx)
    loads[0].wait()
    loads[1].wait()

    for t in range(nctx // 2):
        columns = slice(2 * t * HD, 2 * (t + 1) * HD)
        k_two, v_two = k_ref[:, columns], v_ref[:, columns]
        kv_pack[2 * t] = jnp.concatenate([k_two[:, :HD], v_two[:, :HD]], axis=1)
        kv_pack[2 * t + 1] = jnp.concatenate([k_two[:, HD:], v_two[:, HD:]], axis=1)
    meet(nz, nctx)

    def kv_copy(d):
        return plane_copy(
            nz, nctx, d, lambda p: kv_pack.at[p],
            lambda s: kv_ref.at[pl.ds(pl.multiple_of(BLK + s * rows, BLK), rows)], kv_send, kv_recv,
        )

    def kv_go(d, carry):
        kv_copy(d).start()
        return carry

    column_parts = max(1, depth // 256)
    piece_rows = rows * column_parts // nz

    def piece_at(i, begin):
        return (
            pl.ds(pl.multiple_of((i // column_parts) * piece_rows, piece_rows), piece_rows),
            pl.ds(
                pl.multiple_of(
                    begin + core * (depth // 2) + lax.rem(i, column_parts) * 128, 128
                ),
                128,
            ),
        )

    def weight_out(d):
        i = lax.rem(z + d, nz)
        return column_copy(
            i, w_ref.at[piece_at(i, x * depth)], w_all.at[(z // cuts,) + piece_at(i, 0)],
            w_send.at[d], w_recv.at[z // cuts],
        )

    own_piece = pltpu.make_async_copy(
        w_ref.at[piece_at(z, x * depth)], w_all.at[(z // cuts,) + piece_at(z, 0)], own_sem
    )
    is_source = lax.rem(z, cuts) == y

    @pl.when(is_source)
    def _():
        def go(d, carry):
            weight_out(d).start()
            return carry

        lax.fori_loop(1, nz, go, 0)
        own_piece.start()

    lax.fori_loop(1, nctx, kv_go, 0)
    kv_ref[pl.ds(pl.multiple_of(BLK + c * rows, BLK), rows)] = kv_pack[c]

    loads[2].wait()
    loads[3].wait()
    for t in range(nctx // 2):
        columns = slice(2 * t * HD, 2 * (t + 1) * HD)
        top, bottom = q_ref[:BLK, columns], q_ref[BLK:, columns]
        q_pack[2 * t] = jnp.concatenate([top[:, :HD], bottom[:, :HD]], axis=1)
        q_pack[2 * t + 1] = jnp.concatenate([top[:, HD:], bottom[:, HD:]], axis=1)

    for s in range(cuts):

        @pl.when(z != s * cuts + y)
        def _():
            column_copy(
                lax.rem(z + 1, nz), w_ref.at[piece_at(z, x * depth)], w_all.at[(s,) + piece_at(z, 0)],
                w_send.at[0], w_recv.at[s],
            ).wait_recv()

    @pl.when(is_source)
    def _():
        own_piece.wait()

    def weight_copy(d, incoming=False):
        at = w_all.at[
            (slice(None),) + piece_at(lax.rem(z - d + nz, nz) if incoming else z, 0)
        ]
        return column_copy(lax.rem(z + d, nz), at, at, a_send.at[d], a_recv.at[d])

    def weight_go(d, carry):
        weight_copy(d).start()
        return carry

    lax.fori_loop(1, nz, weight_go, 0)

    devices = nz * nctx
    count[...] = jnp.zeros_like(count)
    span = 2 * pos_ref.shape[1]
    group_ids = lax.broadcasted_iota(jnp.int32, (devices, span), 0)
    inside_ids = lax.broadcasted_iota(jnp.int32, (rows, span), 0)

    def tally(i, carry):
        pos = jnp.concatenate([pos_ref[pl.ds(2 * i, 1), :], pos_ref[pl.ds(2 * i + 1, 1), :]], axis=1)
        group = pos // rows
        inside = pos - group * rows
        hit = jnp.where(group_ids == group, 1.0, 0.0).astype(jnp.bfloat16)
        spot = jnp.where(inside_ids == inside, 1.0, 0.0).astype(jnp.bfloat16)
        count[...] += contract(hit, spot, 1, 1)
        return carry

    lax.fori_loop(0, pos_ref.shape[0] // 2, tally, 0)
    masked = jnp.where(count[...] > 0.5, 1.0, 0.0)
    before = lax.broadcasted_iota(jnp.int32, (rows, rows), 0) < lax.broadcasted_iota(
        jnp.int32, (rows, rows), 1
    )
    rank = contract(masked.astype(jnp.bfloat16), jnp.where(before, 1.0, 0.0).astype(jnp.bfloat16), 1, 0)
    count[...] = jnp.where(masked > 0.5, rank, -1.0)
    most = jnp.max(jnp.max(count[...], axis=0, keepdims=True), axis=1, keepdims=True)
    most_ref[0, 0] = jnp.max(most)
    rank_ref[...] = count[pl.ds(pl.multiple_of(z * nctx, nctx), nctx), :]
    mine = chosen(rank_ref[pl.ds(c, 1), :])
    up_own[...] = contract(mine, ct_ref[...], 1, 0).astype(jnp.bfloat16)

    def share(i):
        return pl.ds(pl.multiple_of(i * depth, depth), depth)

    def up_copy(d):
        target = lax.rem(chip + d, nctx // 2)
        return pltpu.make_async_remote_copy(
            src_ref=up_own.at[:, share(target // cuts)],
            dst_ref=up_all.at[pl.ds(pl.multiple_of(chip * CAP, CAP), CAP)],
            send_sem=up_send,
            recv_sem=up_recv,
            device_id=(z, 2 * target + core),
            device_id_type=MESH,
        )

    def up_go(d, carry):
        up_copy(d).start()
        return carry

    lax.fori_loop(1, nctx // 2, up_go, 0)
    up_all[pl.ds(pl.multiple_of(chip * CAP, CAP), CAP)] = up_own[:, share(x)]

    def q_go(d, carry):
        plane_copy(
            nz, nctx, d, lambda p: q_pack.at[p], lambda s: q_all.at[s], q_send, q_recv
        ).start()
        return carry

    lax.fori_loop(1, nctx, q_go, 0)
    q_all[c] = q_pack[c]

    all_of(kv_ref.at[pl.ds(0, (nctx - 1) * rows)], kv_send, kv_recv).wait_recv()
    low_edge = kv_ref.at[pl.ds(0, BLK)]
    high_edge = kv_ref.at[pl.ds((local_blocks + 1) * BLK, BLK)]
    down, up = edge_copies(
        nz, kv_ref.at[pl.ds(BLK, BLK)], high_edge, kv_ref.at[pl.ds(local_blocks * BLK, BLK)],
        low_edge, edge_send, edge_recv,
    )
    wanted = [glob_ref[i] - z * local_blocks for i in range(GLOB)]

    def pick(b, totals):
        block = kv_ref[pl.ds(pl.multiple_of(BLK + b * BLK, BLK), BLK), :]
        return tuple(
            jnp.where(jnp.full(block.shape, wanted[i] == b), block, totals[i]) for i in range(GLOB)
        )

    nothing = jnp.zeros((BLK, 2 * HD), jnp.bfloat16)
    picked = lax.fori_loop(0, local_blocks, pick, (nothing,) * GLOB, unroll=8)
    g_own[...] = jnp.concatenate(picked, axis=0)
    stage_in = inner_copies(nz, nctx, side, g_own, g_in, in_send, in_recv)
    for copy in stage_in:
        copy.start()

    @pl.when(z > 0)
    def _():
        down.start()

    @pl.when(z < nz - 1)
    def _():
        up.start()

    half = pl.ds(pl.multiple_of(core * (depth // 2), depth // 2), depth // 2)
    other_half = pl.ds(pl.multiple_of((1 - core) * (depth // 2), depth // 2), depth // 2)

    def pair_copy(src, dst, i):
        return pltpu.make_async_remote_copy(
            src_ref=src,
            dst_ref=dst,
            send_sem=pair_send.at[i],
            recv_sem=pair_recv.at[i],
            device_id=(z, partner),
            device_id_type=MESH,
        )

    cross_out = pair_copy(w_all.at[:, :, half], w_all.at[:, :, half], 0)
    cross_in = pair_copy(w_all.at[:, :, other_half], w_all.at[:, :, other_half], 0)

    def weight_in(d, carry):
        weight_copy(d, True).wait_recv()
        return carry

    lax.fori_loop(1, nz, weight_in, 0)
    cross_out.start()

    total = g_own[...].astype(jnp.float32)
    for e, copy in enumerate(stage_in):
        copy.wait_recv()
        total = total + g_in[e + 1].astype(jnp.float32)
    g_mid[...] = total.astype(jnp.bfloat16)
    stage_out = outer_copies(nz, nctx, side, g_mid, g_out, out_send, out_recv)
    for copy in stage_out:
        copy.start()

    all_of(up_all.at[pl.ds(0, (nctx // 2 - 1) * CAP)], up_send, up_recv).wait_recv()
    cross_in.wait_recv()
    for s in range(cuts):
        p_out[s] = contract(up_all[...], w_all[s], 1, 1)

    def partial_copy(e):
        target = lax.rem(x + e, cuts)
        return pltpu.make_async_remote_copy(
            src_ref=p_out.at[target],
            dst_ref=p_in.at[e],
            send_sem=p_send.at[e],
            recv_sem=p_recv.at[e],
            device_id=(z, 2 * (target * cuts + y) + core),
            device_id_type=MESH,
        )

    partials = [partial_copy(e) for e in range(1, cuts)]
    for copy in partials:
        copy.start()

    @pl.when(z > 0)
    def _():
        column_copy(jnp.maximum(z - 1, 0), low_edge, low_edge, edge_send.at[1], edge_recv.at[1]).wait_recv()

    @pl.when(z == 0)
    def _():
        kv_ref[pl.ds(0, BLK), :] = nothing

    @pl.when(z < nz - 1)
    def _():
        column_copy(
            jnp.minimum(z + 1, nz - 1), high_edge, high_edge, edge_send.at[0], edge_recv.at[0]
        ).wait_recv()

    @pl.when(z == nz - 1)
    def _():
        kv_ref[pl.ds((local_blocks + 1) * BLK, BLK), :] = nothing

    total = g_mid[...].astype(jnp.float32)
    for e, copy in enumerate(stage_out):
        copy.wait_recv()
        total = total + g_out[e + 1].astype(jnp.float32)
    kv_ref[pl.ds((local_blocks + 2) * BLK, GLOB * BLK), :] = total.astype(jnp.bfloat16)

    all_of(q_all.at[pl.ds(0, nctx - 1)], q_send, q_recv).wait_recv()
    low_rows = lax.broadcasted_iota(jnp.int32, (rows, 2 * HD), 1) < HD

    def lay(j, carry):
        two = q_all[j]
        begin = pl.multiple_of(j * rows, rows)
        qg_ref[pl.ds(begin, BLK), :] = two
        qg_ref[pl.ds(begin + BLK, BLK), :] = halves(two)
        return carry

    lax.fori_loop(0, nctx, lay, 0, unroll=4)
    grad = p_out[x]
    for e, copy in enumerate(partials):
        copy.wait_recv()
        grad = grad + p_in[e + 1]
    g_all[core] = grad.astype(jnp.bfloat16)
    swap_out = pair_copy(g_all.at[core], g_all.at[core], 1)
    swap_in = pair_copy(g_all.at[1 - core], g_all.at[1 - core], 1)
    swap_out.start()
    swap_in.wait_recv()

    def expand(j, carry):
        marks = chosen(rank_ref[pl.ds(j, 1), :])
        compact = g_all[lax.rem(j, 2), pl.ds(pl.multiple_of((j // 2) * CAP, CAP), CAP), :]
        dense = contract(marks, compact, 0, 0).astype(jnp.bfloat16)
        dense = jnp.where(jnp.full(dense.shape, core == 0), halves(dense), dense)
        at = pl.ds(pl.multiple_of(j * rows, rows), rows)
        qg_ref[at, :] = jnp.where(low_rows, qg_ref[at, :], dense)
        return carry

    lax.fori_loop(0, nctx, expand, 0, unroll=4)

    all_of(kv_pack.at[pl.ds(0, nctx - 1)], kv_send, kv_recv).wait_send()
    all_of(q_pack.at[pl.ds(0, nctx - 1)], q_send, q_recv).wait_send()
    all_of(up_all.at[pl.ds(0, (nctx // 2 - 1) * CAP)], up_send, up_recv).wait_send()

    def left_weight(d, carry):
        weight_copy(d).wait_send()

        @pl.when(is_source)
        def _():
            weight_out(d).wait_send()

        return carry

    lax.fori_loop(1, nz, left_weight, 0)

    @pl.when(z > 0)
    def _():
        down.wait_send()

    @pl.when(z < nz - 1)
    def _():
        up.wait_send()

    for copy in stage_in + stage_out + partials:
        copy.wait_send()
    cross_out.wait_send()
    swap_out.wait_send()


def collect(nz, nctx, global_blocks, q, k, v, ct, w, positions):
    rows, wide = q.shape
    region = nctx * rows
    side, cuts = square(nz), square(nctx // 2)
    half = jnp.bfloat16
    dma = pltpu.SemaphoreType.DMA
    vmem = pl.BlockSpec(memory_space=pltpu.VMEM)
    return pl.pallas_call(
        functools.partial(collect_kernel, nz, nctx),
        out_shape=(
            jax.ShapeDtypeStruct((region + (2 + GLOB) * BLK, 2 * HD), half),
            jax.ShapeDtypeStruct((region, 2 * HD), half),
            jax.ShapeDtypeStruct((nctx, rows), jnp.float32),
            jax.ShapeDtypeStruct((1, 1), jnp.float32),
        ),
        in_specs=[pl.BlockSpec(memory_space=pltpu.SMEM)]
        + [pl.BlockSpec(memory_space=pl.ANY)] * 5
        + [vmem],
        out_specs=(vmem, vmem, vmem, pl.BlockSpec(memory_space=pltpu.SMEM)),
        scratch_shapes=[
            pltpu.VMEM((nctx, rows, 2 * HD), half),
            pltpu.VMEM((nctx, BLK, 2 * HD), half),
            pltpu.VMEM((nctx, BLK, 2 * HD), half),
            pltpu.VMEM((CAP, wide), half),
            pltpu.VMEM((nctx // 2 * CAP, wide // cuts), half),
            pltpu.VMEM((cuts, rows, wide // cuts), half),
            pltpu.VMEM((cuts, nctx // 2 * CAP, 2 * HD), jnp.float32),
            pltpu.VMEM((cuts, nctx // 2 * CAP, 2 * HD), jnp.float32),
            pltpu.VMEM((2, nctx // 2 * CAP, 2 * HD), half),
            pltpu.VMEM((nz * nctx, rows), jnp.float32),
            pltpu.VMEM((GLOB * BLK, 2 * HD), half),
            pltpu.VMEM((side, GLOB * BLK, 2 * HD), half),
            pltpu.VMEM((GLOB * BLK, 2 * HD), half),
            pltpu.VMEM((nz // side, GLOB * BLK, 2 * HD), half),
            dma(()), dma(()), dma(()), dma(()), dma(()), dma(()),
            dma((nz,)), dma((cuts,)), dma((nz,)), dma((nz,)), dma((cuts,)), dma((cuts,)),
            dma((2,)), dma((2,)),
            dma((side,)), dma((side,)), dma((nz // side,)), dma((nz // side,)),
            dma((2,)), dma((2,)), dma(()),
            pltpu.VMEM((rows, wide), half), pltpu.VMEM((rows, wide), half),
            pltpu.VMEM((rows, wide), half), pltpu.VMEM((rows, wide), half), dma((4,)),
        ],
        compiler_params=pltpu.CompilerParams(
            collective_id=0, has_side_effects=True, vmem_limit_bytes=56 * 1024 * 1024
        ),
        name="collect",
    )(global_blocks, q, k, v, ct, w, positions.reshape(-1, 128))


def deliver_kernel(
    nz, nctx, glob_ref, dqo_far, sums_far, rank_ref,
    oq_all, kv_all,
    oq_pack, kv_pack, edge_out, edge_in, g_own, g_in, g_mid, g_out,
    oq_send, oq_recv, kv_send, kv_recv, edge_send, edge_recv, in_send, in_recv, out_send, out_recv,
    dqo_ref, sums_ref, load_sem,
):
    z, c = place(nz, nctx)
    rows = kv_all.shape[1]
    side = square(nz)
    local_blocks = nctx * rows // BLK
    few = CAP // 2
    high_begin = (local_blocks + 1) * BLK
    load_sums = pltpu.make_async_copy(sums_far, sums_ref, load_sem.at[0])
    load_rows = pltpu.make_async_copy(dqo_far, dqo_ref, load_sem.at[1])
    load_sums.start()
    load_rows.start()
    greet(nz, nctx)
    load_sums.wait()
    edge_out[0] = sums_ref[pl.ds(0, BLK), :]
    edge_out[1] = sums_ref[pl.ds(high_begin, BLK), :]
    g_own[...] = sums_ref[pl.ds(high_begin + BLK, GLOB * BLK), :]

    load_rows.wait()

    def shrink(j, carry):
        both = dqo_ref[pl.ds(pl.multiple_of(j * rows, rows), rows), :]
        oq_pack[j, pl.ds(0, BLK), :] = jnp.concatenate([both[:BLK, HD:], both[BLK:, HD:]], axis=1)
        picked = contract(chosen(rank_ref[pl.ds(j, 1), :]), both, 1, 0).astype(jnp.bfloat16)
        oq_pack[j, pl.ds(BLK, few), :] = jnp.concatenate([picked[:few, :HD], picked[few:, :HD]], axis=1)
        return carry

    lax.fori_loop(0, nctx, shrink, 0, unroll=4)
    meet(nz, nctx)
    stage_in = inner_copies(nz, nctx, side, g_own, g_in, in_send, in_recv)
    for copy in stage_in:
        copy.start()
    down, up = edge_copies(
        nz, edge_out.at[0], edge_in.at[0], edge_out.at[1], edge_in.at[1], edge_send, edge_recv
    )

    @pl.when(z > 0)
    def _():
        down.start()

    @pl.when(z < nz - 1)
    def _():
        up.start()

    def oq_go(d, carry):
        plane_copy(
            nz, nctx, d, lambda p: oq_pack.at[p], lambda s: oq_all.at[s], oq_send, oq_recv
        ).start()
        return carry

    lax.fori_loop(1, nctx, oq_go, 0)
    oq_all[c] = oq_pack[c]

    total = g_own[...].astype(jnp.float32)
    for e, copy in enumerate(stage_in):
        copy.wait_recv()
        total = total + g_in[e + 1].astype(jnp.float32)
    g_mid[...] = total.astype(jnp.bfloat16)
    stage_out = outer_copies(nz, nctx, side, g_mid, g_out, out_send, out_recv)
    for copy in stage_out:
        copy.start()

    @pl.when(z > 0)
    def _():
        column_copy(
            jnp.maximum(z - 1, 0), edge_out.at[1], edge_in.at[1], edge_send.at[1], edge_recv.at[1]
        ).wait_recv()

    @pl.when(z == 0)
    def _():
        edge_in[1] = jnp.zeros_like(edge_in[1])

    @pl.when(z < nz - 1)
    def _():
        column_copy(
            jnp.minimum(z + 1, nz - 1), edge_out.at[0], edge_in.at[0], edge_send.at[0], edge_recv.at[0]
        ).wait_recv()

    @pl.when(z == nz - 1)
    def _():
        edge_in[0] = jnp.zeros_like(edge_in[0])

    for copy in stage_out:
        copy.wait_recv()
    for e in range(1, nz // side):
        total = total + g_out[e].astype(jnp.float32)
    wanted = [glob_ref[i] - z * local_blocks for i in range(GLOB)]

    def settle(j):
        for side_of in range(2):
            b = 2 * j + side_of
            term = sums_ref[pl.ds(pl.multiple_of((b + 1) * BLK, BLK), BLK), :].astype(jnp.float32)
            for i in range(GLOB):
                extra = total[i * BLK : (i + 1) * BLK]
                term = term + jnp.where(jnp.full(extra.shape, wanted[i] == b), extra, 0.0)
            edge = edge_in[1 - side_of].astype(jnp.float32)
            at_edge = j == (nctx - 1) * side_of
            term = term + jnp.where(jnp.full(edge.shape, at_edge), edge, 0.0)
            kv_pack[j, pl.ds(side_of * BLK, BLK), :] = term.astype(jnp.bfloat16)

    def kv_go(d, carry):
        settle(lax.rem(c + d, nctx))
        plane_copy(
            nz, nctx, d, lambda p: kv_pack.at[p], lambda s: kv_all.at[s], kv_send, kv_recv
        ).start()
        return carry

    lax.fori_loop(1, nctx, kv_go, 0)
    settle(c)
    kv_all[c] = kv_pack[c]

    all_of(oq_all.at[pl.ds(0, nctx - 1)], oq_send, oq_recv).wait_recv()
    all_of(kv_all.at[pl.ds(0, nctx - 1)], kv_send, kv_recv).wait_recv()
    all_of(oq_pack.at[pl.ds(0, nctx - 1)], oq_send, oq_recv).wait_send()
    all_of(kv_pack.at[pl.ds(0, nctx - 1)], kv_send, kv_recv).wait_send()

    @pl.when(z > 0)
    def _():
        down.wait_send()

    @pl.when(z < nz - 1)
    def _():
        up.wait_send()

    for copy in stage_in + stage_out:
        copy.wait_send()


def deliver(nz, nctx, rows, global_blocks, dqo, sums, rank):
    side = square(nz)
    half = jnp.bfloat16
    dma = pltpu.SemaphoreType.DMA
    vmem = pl.BlockSpec(memory_space=pltpu.VMEM)
    return pl.pallas_call(
        functools.partial(deliver_kernel, nz, nctx),
        out_shape=(
            jax.ShapeDtypeStruct((nctx, BLK + CAP // 2, 2 * HD), half),
            jax.ShapeDtypeStruct((nctx, rows, 2 * HD), half),
        ),
        in_specs=[pl.BlockSpec(memory_space=pltpu.SMEM)]
        + [pl.BlockSpec(memory_space=pl.ANY)] * 2
        + [vmem],
        out_specs=(vmem,) * 2,
        scratch_shapes=[
            pltpu.VMEM((nctx, BLK + CAP // 2, 2 * HD), half),
            pltpu.VMEM((nctx, rows, 2 * HD), half),
            pltpu.VMEM((2, BLK, 2 * HD), half),
            pltpu.VMEM((2, BLK, 2 * HD), half),
            pltpu.VMEM((GLOB * BLK, 2 * HD), half),
            pltpu.VMEM((side, GLOB * BLK, 2 * HD), half),
            pltpu.VMEM((GLOB * BLK, 2 * HD), half),
            pltpu.VMEM((nz // side, GLOB * BLK, 2 * HD), half),
            dma(()), dma(()), dma(()), dma(()),
            dma((2,)), dma((2,)),
            dma((side,)), dma((side,)), dma((nz // side,)), dma((nz // side,)),
            pltpu.VMEM(dqo.shape, half), pltpu.VMEM(sums.shape, half), dma((2,)),
        ],
        compiler_params=pltpu.CompilerParams(
            collective_id=1, has_side_effects=True, vmem_limit_bytes=56 * 1024 * 1024
        ),
        name="deliver",
    )(global_blocks, dqo, sums, rank)


def spread_kernel(oq_ref, kv_ref, rank_ref, most_ref, full_ref, o_ref, dq_ref, dk_ref, dv_ref, compact):
    few = CAP // 2
    for t in range(oq_ref.shape[0] // 2):
        columns = slice(2 * t * HD, 2 * (t + 1) * HD)
        first, second = oq_ref[2 * t], oq_ref[2 * t + 1]
        o_ref[:BLK, columns] = jnp.concatenate([first[:BLK, :HD], second[:BLK, :HD]], axis=1)
        o_ref[BLK:, columns] = jnp.concatenate([first[:BLK, HD:], second[:BLK, HD:]], axis=1)
        compact[:few, columns] = jnp.concatenate([first[BLK:, :HD], second[BLK:, :HD]], axis=1)
        compact[few:, columns] = jnp.concatenate([first[BLK:, HD:], second[BLK:, HD:]], axis=1)
        first, second = kv_ref[2 * t], kv_ref[2 * t + 1]
        dk_ref[:, columns] = jnp.concatenate([first[:, :HD], second[:, :HD]], axis=1)
        dv_ref[:, columns] = jnp.concatenate([first[:, HD:], second[:, HD:]], axis=1)
    marks = chosen(rank_ref[pl.ds(lax.axis_index("ctx"), 1), :])
    spread = contract(marks, compact[...], 0, 0).astype(jnp.bfloat16)
    crowded = jnp.full(spread.shape, most_ref[0, 0]) > CAP - 0.5
    dq_ref[...] = jnp.where(crowded, full_ref[...], spread)


def spread(oq, kv, rank, most, full):
    vmem = pl.BlockSpec(memory_space=pltpu.VMEM)
    return pl.pallas_call(
        spread_kernel,
        out_shape=(jax.ShapeDtypeStruct(full.shape, full.dtype),) * 4,
        in_specs=[vmem, vmem, vmem, pl.BlockSpec(memory_space=pltpu.SMEM), vmem],
        out_specs=(vmem,) * 4,
        scratch_shapes=[pltpu.VMEM((CAP, full.shape[1]), full.dtype)],
        compiler_params=pltpu.CompilerParams(vmem_limit_bytes=48 * 1024 * 1024),
        name="spread",
    )(oq, kv, rank, most, full)


def body(queries, keys, values, out_weight, cotangent, positions, global_blocks, random_blocks):
    rows_here = queries.shape[0]
    nz, nctx = lax.axis_size("fsdp"), lax.axis_size("ctx")
    local_blocks = nctx * rows_here // BLK
    kv, qg, rank, most = collect(
        nz, nctx, global_blocks, queries, keys, values, cotangent, out_weight, positions
    )
    crowded = most[0, 0] > CAP - 0.5

    def dense_gradient(qg):
        offset = (lax.axis_index("fsdp") * nctx + lax.axis_index("ctx")) * rows_here
        places = offset + jnp.arange(rows_here, dtype=jnp.int32)
        masked = jnp.any(positions[:, None] == places[None, :], axis=0)
        upstream = jnp.where(masked[:, None], cotangent, jnp.zeros_like(cotangent))
        weight = lax.all_gather(out_weight, "fsdp", axis=0, tiled=True)
        grad = contract(upstream, weight, 1, 1).astype(jnp.bfloat16)
        grad = lax.all_to_all(grad, "ctx", split_axis=1, concat_axis=0, tiled=True)
        return jnp.concatenate([qg[:, :HD], grad], axis=1)

    qg = lax.cond(crowded, dense_gradient, lambda qg: qg, qg)
    picks = random_blocks.transpose(2, 1, 0).reshape(random_blocks.shape[2], local_blocks)
    dqo, sums = attend(global_blocks, picks, kv, qg)
    parts, key_values = deliver(nz, nctx, rows_here, global_blocks, dqo, sums, rank)

    def dense_query():
        return lax.all_to_all(dqo[:, :HD], "ctx", split_axis=0, concat_axis=1, tiled=True)

    full = lax.cond(crowded, dense_query, lambda: jnp.zeros_like(queries))
    return spread(parts, key_values, rank, most, full)


def solution(mesh):
    split = P(("fsdp", "ctx"), None)
    return jax.shard_map(
        body,
        mesh=mesh,
        in_specs=(split, split, split, P("fsdp", None), split, P(), P(), P("fsdp", "ctx", None)),
        out_specs=(split, split, split, split),
        check_vma=False,
    )
```

```python
import functools
import math

import jax
import jax.numpy as jnp
from jax import lax
from jax.experimental import pallas as pl
from jax.experimental.pallas import tpu as pltpu
from jax.sharding import PartitionSpec as P

HD = 64
BLK = 64
GLOB = 2
SLOTS = 8


def contract(a, b, da, db):
    return lax.dot_general(a, b, (((da,), (db,)), ((), ())), preferred_element_type=jnp.float32)


def attend_kernel(glob_ref, pick_ref, kv_ref, qg_ref, dqo_ref, sum_ref, dkv_ref):
    width = 2 * HD
    scale = math.log2(math.e) / math.sqrt(HD)
    low = lax.broadcasted_iota(jnp.int32, (BLK, width), 1) < HD
    zero = jnp.zeros((BLK, width), jnp.bfloat16)
    dkv_ref[...] = jnp.zeros_like(dkv_ref)
    blocks = kv_ref.shape[0] // BLK
    local_blocks = qg_ref.shape[0] // BLK
    first_block = lax.axis_index("fsdp") * local_blocks
    last_block = local_blocks * lax.axis_size("fsdp") - 1
    lower = lax.broadcasted_iota(jnp.int32, (1, width), 1) < HD

    def candidates(i):
        current = first_block + i
        far = [glob_ref[g] for g in range(GLOB)] + [pick_ref[r, i] for r in range(SLOTS - 3 - GLOB)]
        usable = [current > 0, current >= 0, current < last_block]
        for n, block in enumerate(far):
            good = jnp.abs(block - current) > 1
            for earlier in far[:n]:
                good = jnp.logical_and(good, block != earlier)
            usable.append(good)
        ids = [i, i + 1, i + 2] + [blocks - GLOB + g for g in range(GLOB)]
        ids += [block - first_block + 1 for block in far[GLOB:]]
        return ids, [jnp.where(good, 0.0, -1e30) for good in usable]

    def rows(block):
        return pl.ds(pl.multiple_of(block * BLK, BLK), BLK)

    def step(j, carry):
        first = qg_ref[rows(2 * j), :]
        second = qg_ref[rows(2 * j + 1), :]
        mixed = jnp.concatenate(
            [
                jnp.concatenate([jnp.where(low, first, zero), zero], axis=1),
                jnp.concatenate([zero, jnp.where(low, second, zero)], axis=1),
                jnp.concatenate([jnp.where(low, zero, first), zero], axis=1),
                jnp.concatenate([zero, jnp.where(low, zero, second)], axis=1),
            ],
            axis=0,
        )
        left, left_bias = candidates(2 * j)
        right, right_bias = candidates(2 * j + 1)
        both = jnp.concatenate(
            [
                jnp.concatenate([kv_ref[rows(a), :], kv_ref[rows(b), :]], axis=1)
                for a, b in zip(left, right)
            ],
            axis=0,
        )
        products = contract(both, mixed, 1, 1)
        scores = []
        for s in range(SLOTS):
            part = products[s * BLK : (s + 1) * BLK, :width]
            scores.append(part * scale + jnp.where(lower, left_bias[s], right_bias[s]))
        highest = functools.reduce(jnp.maximum, scores)
        highest = jnp.max(highest, axis=0, keepdims=True)
        raised = [jnp.exp2(part - highest) for part in scores]
        total = jnp.sum(functools.reduce(jnp.add, raised), axis=0, keepdims=True)
        inverse = 1.0 / total
        probs = [part * inverse for part in raised]
        grads = [products[s * BLK : (s + 1) * BLK, width:] for s in range(SLOTS)]
        inner = functools.reduce(jnp.add, [p * g for p, g in zip(probs, grads)])
        inner = jnp.sum(inner, axis=0, keepdims=True)
        weights = jnp.concatenate(
            [
                jnp.concatenate(
                    [(p * (g - inner)).astype(jnp.bfloat16), p.astype(jnp.bfloat16)], axis=1
                )
                for p, g in zip(probs, grads)
            ],
            axis=0,
        )
        sums = contract(weights, both, 0, 0)
        eighth = jnp.where(low, 1.0 / math.sqrt(HD), 1.0)
        out_first = jnp.where(low, sums[:BLK, :width], sums[2 * BLK : 3 * BLK, :width]) * eighth
        out_second = jnp.where(low, sums[BLK : 2 * BLK, width:], sums[3 * BLK :, width:]) * eighth
        dqo_ref[rows(2 * j), :] = out_first.astype(jnp.bfloat16)
        dqo_ref[rows(2 * j + 1), :] = out_second.astype(jnp.bfloat16)
        terms = contract(weights, mixed, 1, 0)

        def term(s, side):
            return terms[s * BLK : (s + 1) * BLK, side * width : (side + 1) * width]

        dkv_ref[rows(2 * j), :] += term(0, 0)
        dkv_ref[rows(2 * j + 1), :] += term(1, 0) + term(0, 1)
        dkv_ref[rows(2 * j + 2), :] += term(2, 0) + term(1, 1)
        dkv_ref[rows(2 * j + 3), :] += term(2, 1)
        for s in range(3, 3 + GLOB):
            dkv_ref[rows(blocks - GLOB + s - 3), :] += term(s, 0) + term(s, 1)
        for s in range(3 + GLOB, SLOTS):
            dkv_ref[rows(left[s]), :] += term(s, 0)
            dkv_ref[rows(right[s]), :] += term(s, 1)
        return carry

    lax.fori_loop(0, local_blocks // 2, step, 0, unroll=2)
    eighth = jnp.where(low, 1.0 / math.sqrt(HD), 1.0)

    def finish(b, carry):
        sum_ref[rows(b), :] = (dkv_ref[rows(b), :] * eighth).astype(jnp.bfloat16)
        return carry

    lax.fori_loop(0, blocks, finish, 0, unroll=4)


def attend(global_blocks, picks, kv, qg):
    smem, vmem = pl.BlockSpec(memory_space=pltpu.SMEM), pl.BlockSpec(memory_space=pltpu.VMEM)
    return pl.pallas_call(
        attend_kernel,
        out_shape=(
            jax.ShapeDtypeStruct(qg.shape, jnp.bfloat16),
            jax.ShapeDtypeStruct(kv.shape, jnp.bfloat16),
        ),
        in_specs=[smem, smem, vmem, vmem],
        out_specs=(vmem, vmem),
        scratch_shapes=[pltpu.VMEM(kv.shape, jnp.float32)],
        compiler_params=pltpu.CompilerParams(vmem_limit_bytes=48 * 1024 * 1024),
        name="attend",
    )(global_blocks, picks, kv, qg)


CAP = 32
MESH = pl.DeviceIdType.MESH


def place(nz, nctx):
    z = lax.axis_index("fsdp")
    c = lax.axis_index("ctx")
    return z, c


def greet(nz, nctx):
    z, c = place(nz, nctx)
    barrier = pltpu.get_barrier_semaphore()

    def plane(d, carry):
        peer = lax.rem(c + d, nctx)
        pl.semaphore_signal(barrier, inc=1, device_id=(z, peer), device_id_type=MESH)
        return carry

    def column(d, carry):
        peer = lax.rem(z + d, nz)
        pl.semaphore_signal(barrier, inc=1, device_id=(peer, c), device_id_type=MESH)
        return carry

    lax.fori_loop(1, nctx, plane, 0)
    lax.fori_loop(1, nz, column, 0)


def meet(nz, nctx):
    pl.semaphore_wait(pltpu.get_barrier_semaphore(), nctx + nz - 2)


def plane_copy(nz, nctx, d, src, dst, send, recv):
    z, c = place(nz, nctx)
    peer = lax.rem(c + d, nctx)
    return pltpu.make_async_remote_copy(
        src_ref=src(peer),
        dst_ref=dst(c),
        send_sem=send,
        recv_sem=recv,
        device_id=(z, peer),
        device_id_type=MESH,
    )


def all_of(view, send, recv):
    z, c = lax.axis_index("fsdp"), lax.axis_index("ctx")
    return pltpu.make_async_remote_copy(
        src_ref=view,
        dst_ref=view,
        send_sem=send,
        recv_sem=recv,
        device_id=(z, lax.bitwise_xor(c, 1)),
        device_id_type=MESH,
    )


def column_copy(peer, src, dst, send, recv):
    c = lax.axis_index("ctx")
    return pltpu.make_async_remote_copy(
        src_ref=src,
        dst_ref=dst,
        send_sem=send,
        recv_sem=recv,
        device_id=(peer, c),
        device_id_type=MESH,
    )


def inner_copies(nz, nctx, side, src, buf, send, recv):
    z, c = place(nz, nctx)
    group, member = z // side, lax.rem(z, side)
    return [
        column_copy(
            group * side + lax.rem(member + e, side), src, buf.at[e], send.at[e], recv.at[e]
        )
        for e in range(1, side)
    ]


def outer_copies(nz, nctx, side, src, buf, send, recv):
    z, c = place(nz, nctx)
    group, member = z // side, lax.rem(z, side)
    groups = nz // side
    return [
        column_copy(
            lax.rem(group + e, groups) * side + member, src, buf.at[e], send.at[e], recv.at[e]
        )
        for e in range(1, groups)
    ]


def edge_copies(nz, down_src, down_dst, up_src, up_dst, send, recv):
    z = lax.axis_index("fsdp")
    down = column_copy(jnp.maximum(z - 1, 0), down_src, down_dst, send.at[0], recv.at[0])
    up = column_copy(jnp.minimum(z + 1, nz - 1), up_src, up_dst, send.at[1], recv.at[1])
    return down, up


def halves(x):
    return jnp.concatenate([x[:, HD:], x[:, :HD]], axis=1)


def chosen(rank_row):
    order = lax.broadcasted_iota(jnp.int32, (CAP, rank_row.shape[1]), 0).astype(jnp.float32)
    return jnp.where(order == rank_row, 1.0, 0.0).astype(jnp.bfloat16)


def square(n):
    return max(s for s in range(1, n + 1) if s * s <= n)


def collect_kernel(
    nz, nctx, glob_ref, q_far, k_far, v_far, ct_far, w_ref, pos_ref,
    kv_ref, qg_ref, rank_ref, most_ref,
    kv_pack, q_pack, q_all, up_own, up_all, w_all, p_out, p_in, g_all, count, g_own, g_in, g_mid, g_out,
    kv_send, kv_recv, q_send, q_recv, up_send, up_recv, w_send, w_recv, a_send, a_recv, p_send, p_recv,
    edge_send, edge_recv, in_send, in_recv, out_send, out_recv, pair_send, pair_recv, own_sem,
    q_ref, k_ref, v_ref, ct_ref, load_sem,
):
    z, c = place(nz, nctx)
    chip, core = c // 2, lax.rem(c, 2)
    cuts = square(nctx // 2)
    x, y = chip // cuts, lax.rem(chip, cuts)
    loads = [
        pltpu.make_async_copy(far, near, load_sem.at[i])
        for i, (far, near) in enumerate(
            [(k_far, k_ref), (v_far, v_ref), (q_far, q_ref), (ct_far, ct_ref)]
        )
    ]
    for load in loads:
        load.start()
    rows = q_ref.shape[0]
    wide = q_ref.shape[1]
    depth = wide // cuts
    side = square(nz)
    local_blocks = nctx * rows // BLK
    partner = 2 * chip + 1 - core
    low = lax.broadcasted_iota(jnp.int32, (BLK, 2 * HD), 1) < HD
    greet(nz, nctx)
    loads[0].wait()
    loads[1].wait()

    for t in range(nctx // 2):
        columns = slice(2 * t * HD, 2 * (t + 1) * HD)
        k_two, v_two = k_ref[:, columns], v_ref[:, columns]
        kv_pack[2 * t] = jnp.concatenate([k_two[:, :HD], v_two[:, :HD]], axis=1)
        kv_pack[2 * t + 1] = jnp.concatenate([k_two[:, HD:], v_two[:, HD:]], axis=1)
    meet(nz, nctx)

    def kv_copy(d):
        return plane_copy(
            nz, nctx, d, lambda p: kv_pack.at[p],
            lambda s: kv_ref.at[pl.ds(pl.multiple_of(BLK + s * rows, BLK), rows)], kv_send, kv_recv,
        )

    def kv_go(d, carry):
        kv_copy(d).start()
        return carry

    column_parts = max(1, depth // 256)
    piece_rows = rows * column_parts // nz

    def piece_at(i, begin):
        return (
            pl.ds(pl.multiple_of((i // column_parts) * piece_rows, piece_rows), piece_rows),
            pl.ds(
                pl.multiple_of(
                    begin + core * (depth // 2) + lax.rem(i, column_parts) * 128, 128
                ),
                128,
            ),
        )

    def weight_out(d):
        i = lax.rem(z + d, nz)
        return column_copy(
            i, w_ref.at[piece_at(i, x * depth)], w_all.at[(z // cuts,) + piece_at(i, 0)],
            w_send.at[d], w_recv.at[z // cuts],
        )

    own_piece = pltpu.make_async_copy(
        w_ref.at[piece_at(z, x * depth)], w_all.at[(z // cuts,) + piece_at(z, 0)], own_sem
    )
    is_source = lax.rem(z, cuts) == y

    @pl.when(is_source)
    def _():
        def go(d, carry):
            weight_out(d).start()
            return carry

        lax.fori_loop(1, nz, go, 0)
        own_piece.start()

    lax.fori_loop(1, nctx, kv_go, 0)
    kv_ref[pl.ds(pl.multiple_of(BLK + c * rows, BLK), rows)] = kv_pack[c]

    loads[2].wait()
    loads[3].wait()
    for t in range(nctx // 2):
        columns = slice(2 * t * HD, 2 * (t + 1) * HD)
        top, bottom = q_ref[:BLK, columns], q_ref[BLK:, columns]
        q_pack[2 * t] = jnp.concatenate([top[:, :HD], bottom[:, :HD]], axis=1)
        q_pack[2 * t + 1] = jnp.concatenate([top[:, HD:], bottom[:, HD:]], axis=1)

    for s in range(cuts):

        @pl.when(z != s * cuts + y)
        def _():
            column_copy(
                lax.rem(z + 1, nz), w_ref.at[piece_at(z, x * depth)], w_all.at[(s,) + piece_at(z, 0)],
                w_send.at[0], w_recv.at[s],
            ).wait_recv()

    @pl.when(is_source)
    def _():
        own_piece.wait()

    def weight_copy(d, incoming=False):
        at = w_all.at[
            (slice(None),) + piece_at(lax.rem(z - d + nz, nz) if incoming else z, 0)
        ]
        return column_copy(lax.rem(z + d, nz), at, at, a_send.at[d], a_recv.at[d])

    def weight_go(d, carry):
        weight_copy(d).start()
        return carry

    lax.fori_loop(1, nz, weight_go, 0)

    span = 2 * pos_ref.shape[1]
    inside_ids = lax.broadcasted_iota(jnp.int32, (rows, span), 0)
    before = lax.broadcasted_iota(jnp.int32, (rows, rows), 0) < lax.broadcasted_iota(
        jnp.int32, (rows, rows), 1
    )
    before = jnp.where(before, 1.0, 0.0).astype(jnp.bfloat16)

    def tally(i, first, groups):
        pos = jnp.concatenate([pos_ref[pl.ds(2 * i, 1), :], pos_ref[pl.ds(2 * i + 1, 1), :]], axis=1)
        group = pos // rows
        ids = lax.broadcasted_iota(jnp.int32, (groups, span), 0) + first
        hit = jnp.where(ids == group, 1.0, 0.0).astype(jnp.bfloat16)
        spot = jnp.where(inside_ids == pos - group * rows, 1.0, 0.0).astype(jnp.bfloat16)
        return contract(hit, spot, 1, 1)

    def ranks(counts):
        masked = jnp.where(counts > 0.5, 1.0, 0.0)
        return jnp.where(masked > 0.5, contract(masked.astype(jnp.bfloat16), before, 1, 0), -1.0)

    rank_ref[...] = ranks(
        lax.fori_loop(
            0, pos_ref.shape[0] // 2, lambda i, total: total + tally(i, z * nctx, nctx),
            jnp.zeros((nctx, rows), jnp.float32), unroll=4,
        )
    )
    mine = chosen(rank_ref[pl.ds(c, 1), :])
    up_own[...] = contract(mine, ct_ref[...], 1, 0).astype(jnp.bfloat16)

    def share(i):
        return pl.ds(pl.multiple_of(i * depth, depth), depth)

    def up_copy(d):
        target = lax.rem(chip + d, nctx // 2)
        return pltpu.make_async_remote_copy(
            src_ref=up_own.at[:, share(target // cuts)],
            dst_ref=up_all.at[pl.ds(pl.multiple_of(chip * CAP, CAP), CAP)],
            send_sem=up_send,
            recv_sem=up_recv,
            device_id=(z, 2 * target + core),
            device_id_type=MESH,
        )

    def up_go(d, carry):
        up_copy(d).start()
        return carry

    lax.fori_loop(1, nctx // 2, up_go, 0)
    up_all[pl.ds(pl.multiple_of(chip * CAP, CAP), CAP)] = up_own[:, share(x)]

    def q_go(d, carry):
        plane_copy(
            nz, nctx, d, lambda p: q_pack.at[p], lambda s: q_all.at[s], q_send, q_recv
        ).start()
        return carry

    lax.fori_loop(1, nctx, q_go, 0)
    q_all[c] = q_pack[c]

    all_of(kv_ref.at[pl.ds(0, (nctx - 1) * rows)], kv_send, kv_recv).wait_recv()
    low_edge = kv_ref.at[pl.ds(0, BLK)]
    high_edge = kv_ref.at[pl.ds((local_blocks + 1) * BLK, BLK)]
    down, up = edge_copies(
        nz, kv_ref.at[pl.ds(BLK, BLK)], high_edge, kv_ref.at[pl.ds(local_blocks * BLK, BLK)],
        low_edge, edge_send, edge_recv,
    )
    wanted = [glob_ref[i] - z * local_blocks for i in range(GLOB)]

    def pick(b, totals):
        block = kv_ref[pl.ds(pl.multiple_of(BLK + b * BLK, BLK), BLK), :]
        return tuple(
            jnp.where(jnp.full(block.shape, wanted[i] == b), block, totals[i]) for i in range(GLOB)
        )

    nothing = jnp.zeros((BLK, 2 * HD), jnp.bfloat16)
    picked = lax.fori_loop(0, local_blocks, pick, (nothing,) * GLOB, unroll=8)
    g_own[...] = jnp.concatenate(picked, axis=0)
    stage_in = inner_copies(nz, nctx, side, g_own, g_in, in_send, in_recv)
    for copy in stage_in:
        copy.start()

    @pl.when(z > 0)
    def _():
        down.start()

    @pl.when(z < nz - 1)
    def _():
        up.start()

    half = pl.ds(pl.multiple_of(core * (depth // 2), depth // 2), depth // 2)
    other_half = pl.ds(pl.multiple_of((1 - core) * (depth // 2), depth // 2), depth // 2)

    def pair_copy(src, dst, i):
        return pltpu.make_async_remote_copy(
            src_ref=src,
            dst_ref=dst,
            send_sem=pair_send.at[i],
            recv_sem=pair_recv.at[i],
            device_id=(z, partner),
            device_id_type=MESH,
        )

    cross_out = pair_copy(w_all.at[:, :, half], w_all.at[:, :, half], 0)
    cross_in = pair_copy(w_all.at[:, :, other_half], w_all.at[:, :, other_half], 0)

    def weight_in(d, carry):
        weight_copy(d, True).wait_recv()
        return carry

    lax.fori_loop(1, nz, weight_in, 0)
    cross_out.start()

    total = g_own[...].astype(jnp.float32)
    for e, copy in enumerate(stage_in):
        copy.wait_recv()
        total = total + g_in[e + 1].astype(jnp.float32)
    g_mid[...] = total.astype(jnp.bfloat16)
    stage_out = outer_copies(nz, nctx, side, g_mid, g_out, out_send, out_recv)
    for copy in stage_out:
        copy.start()

    all_of(up_all.at[pl.ds(0, (nctx // 2 - 1) * CAP)], up_send, up_recv).wait_recv()
    cross_in.wait_recv()
    for s in range(cuts):
        p_out[s] = contract(up_all[...], w_all[s], 1, 1)

    def partial_copy(e):
        target = lax.rem(x + e, cuts)
        return pltpu.make_async_remote_copy(
            src_ref=p_out.at[target],
            dst_ref=p_in.at[e],
            send_sem=p_send.at[e],
            recv_sem=p_recv.at[e],
            device_id=(z, 2 * (target * cuts + y) + core),
            device_id_type=MESH,
        )

    partials = [partial_copy(e) for e in range(1, cuts)]
    for copy in partials:
        copy.start()

    count[...] = jnp.zeros_like(count)

    def tally_all(i, carry):
        count[...] += tally(i, 0, nz * nctx)
        return carry

    lax.fori_loop(0, pos_ref.shape[0] // 2, tally_all, 0)
    most_ref[0, 0] = jnp.max(ranks(count[...]))

    @pl.when(z > 0)
    def _():
        column_copy(jnp.maximum(z - 1, 0), low_edge, low_edge, edge_send.at[1], edge_recv.at[1]).wait_recv()

    @pl.when(z == 0)
    def _():
        kv_ref[pl.ds(0, BLK), :] = nothing

    @pl.when(z < nz - 1)
    def _():
        column_copy(
            jnp.minimum(z + 1, nz - 1), high_edge, high_edge, edge_send.at[0], edge_recv.at[0]
        ).wait_recv()

    @pl.when(z == nz - 1)
    def _():
        kv_ref[pl.ds((local_blocks + 1) * BLK, BLK), :] = nothing

    total = g_mid[...].astype(jnp.float32)
    for e, copy in enumerate(stage_out):
        copy.wait_recv()
        total = total + g_out[e + 1].astype(jnp.float32)
    kv_ref[pl.ds((local_blocks + 2) * BLK, GLOB * BLK), :] = total.astype(jnp.bfloat16)

    all_of(q_all.at[pl.ds(0, nctx - 1)], q_send, q_recv).wait_recv()
    low_rows = lax.broadcasted_iota(jnp.int32, (rows, 2 * HD), 1) < HD

    def lay(j, carry):
        two = q_all[j]
        begin = pl.multiple_of(j * rows, rows)
        qg_ref[pl.ds(begin, BLK), :] = two
        qg_ref[pl.ds(begin + BLK, BLK), :] = halves(two)
        return carry

    lax.fori_loop(0, nctx, lay, 0, unroll=4)
    grad = p_out[x]
    for e, copy in enumerate(partials):
        copy.wait_recv()
        grad = grad + p_in[e + 1]
    g_all[core] = grad.astype(jnp.bfloat16)
    swap_out = pair_copy(g_all.at[core], g_all.at[core], 1)
    swap_in = pair_copy(g_all.at[1 - core], g_all.at[1 - core], 1)
    swap_out.start()
    swap_in.wait_recv()

    def expand(j, carry):
        marks = chosen(rank_ref[pl.ds(j, 1), :])
        compact = g_all[lax.rem(j, 2), pl.ds(pl.multiple_of((j // 2) * CAP, CAP), CAP), :]
        dense = contract(marks, compact, 0, 0).astype(jnp.bfloat16)
        dense = jnp.where(jnp.full(dense.shape, core == 0), halves(dense), dense)
        at = pl.ds(pl.multiple_of(j * rows, rows), rows)
        qg_ref[at, :] = jnp.where(low_rows, qg_ref[at, :], dense)
        return carry

    lax.fori_loop(0, nctx, expand, 0, unroll=4)

    all_of(kv_pack.at[pl.ds(0, nctx - 1)], kv_send, kv_recv).wait_send()
    all_of(q_pack.at[pl.ds(0, nctx - 1)], q_send, q_recv).wait_send()
    all_of(up_all.at[pl.ds(0, (nctx // 2 - 1) * CAP)], up_send, up_recv).wait_send()

    def left_weight(d, carry):
        weight_copy(d).wait_send()

        @pl.when(is_source)
        def _():
            weight_out(d).wait_send()

        return carry

    lax.fori_loop(1, nz, left_weight, 0)

    @pl.when(z > 0)
    def _():
        down.wait_send()

    @pl.when(z < nz - 1)
    def _():
        up.wait_send()

    for copy in stage_in + stage_out + partials:
        copy.wait_send()
    cross_out.wait_send()
    swap_out.wait_send()


def collect(nz, nctx, global_blocks, q, k, v, ct, w, positions):
    rows, wide = q.shape
    region = nctx * rows
    side, cuts = square(nz), square(nctx // 2)
    half = jnp.bfloat16
    dma = pltpu.SemaphoreType.DMA
    vmem = pl.BlockSpec(memory_space=pltpu.VMEM)
    return pl.pallas_call(
        functools.partial(collect_kernel, nz, nctx),
        out_shape=(
            jax.ShapeDtypeStruct((region + (2 + GLOB) * BLK, 2 * HD), half),
            jax.ShapeDtypeStruct((region, 2 * HD), half),
            jax.ShapeDtypeStruct((nctx, rows), jnp.float32),
            jax.ShapeDtypeStruct((1, 1), jnp.float32),
        ),
        in_specs=[pl.BlockSpec(memory_space=pltpu.SMEM)]
        + [pl.BlockSpec(memory_space=pl.ANY)] * 5
        + [vmem],
        out_specs=(vmem, vmem, vmem, pl.BlockSpec(memory_space=pltpu.SMEM)),
        scratch_shapes=[
            pltpu.VMEM((nctx, rows, 2 * HD), half),
            pltpu.VMEM((nctx, BLK, 2 * HD), half),
            pltpu.VMEM((nctx, BLK, 2 * HD), half),
            pltpu.VMEM((CAP, wide), half),
            pltpu.VMEM((nctx // 2 * CAP, wide // cuts), half),
            pltpu.VMEM((cuts, rows, wide // cuts), half),
            pltpu.VMEM((cuts, nctx // 2 * CAP, 2 * HD), jnp.float32),
            pltpu.VMEM((cuts, nctx // 2 * CAP, 2 * HD), jnp.float32),
            pltpu.VMEM((2, nctx // 2 * CAP, 2 * HD), half),
            pltpu.VMEM((nz * nctx, rows), jnp.float32),
            pltpu.VMEM((GLOB * BLK, 2 * HD), half),
            pltpu.VMEM((side, GLOB * BLK, 2 * HD), half),
            pltpu.VMEM((GLOB * BLK, 2 * HD), half),
            pltpu.VMEM((nz // side, GLOB * BLK, 2 * HD), half),
            dma(()), dma(()), dma(()), dma(()), dma(()), dma(()),
            dma((nz,)), dma((cuts,)), dma((nz,)), dma((nz,)), dma((cuts,)), dma((cuts,)),
            dma((2,)), dma((2,)),
            dma((side,)), dma((side,)), dma((nz // side,)), dma((nz // side,)),
            dma((2,)), dma((2,)), dma(()),
            pltpu.VMEM((rows, wide), half), pltpu.VMEM((rows, wide), half),
            pltpu.VMEM((rows, wide), half), pltpu.VMEM((rows, wide), half), dma((4,)),
        ],
        compiler_params=pltpu.CompilerParams(
            collective_id=0, has_side_effects=True, vmem_limit_bytes=56 * 1024 * 1024
        ),
        name="collect",
    )(global_blocks, q, k, v, ct, w, positions.reshape(-1, 128))


def deliver_kernel(
    nz, nctx, glob_ref, dqo_far, sums_far, rank_ref,
    oq_all, kv_all,
    oq_pack, kv_pack, edge_out, edge_in, g_own, g_in, g_mid, g_out,
    oq_send, oq_recv, kv_send, kv_recv, edge_send, edge_recv, in_send, in_recv, out_send, out_recv,
    dqo_ref, sums_ref, load_sem,
):
    z, c = place(nz, nctx)
    rows = kv_all.shape[1]
    side = square(nz)
    local_blocks = nctx * rows // BLK
    few = CAP // 2
    high_begin = (local_blocks + 1) * BLK
    load_sums = pltpu.make_async_copy(sums_far, sums_ref, load_sem.at[0])
    load_rows = pltpu.make_async_copy(dqo_far, dqo_ref, load_sem.at[1])
    load_sums.start()
    load_rows.start()
    greet(nz, nctx)
    load_sums.wait()
    edge_out[0] = sums_ref[pl.ds(0, BLK), :]
    edge_out[1] = sums_ref[pl.ds(high_begin, BLK), :]
    g_own[...] = sums_ref[pl.ds(high_begin + BLK, GLOB * BLK), :]

    load_rows.wait()

    def shrink(j, carry):
        both = dqo_ref[pl.ds(pl.multiple_of(j * rows, rows), rows), :]
        oq_pack[j, pl.ds(0, BLK), :] = jnp.concatenate([both[:BLK, HD:], both[BLK:, HD:]], axis=1)
        picked = contract(chosen(rank_ref[pl.ds(j, 1), :]), both, 1, 0).astype(jnp.bfloat16)
        oq_pack[j, pl.ds(BLK, few), :] = jnp.concatenate([picked[:few, :HD], picked[few:, :HD]], axis=1)
        return carry

    lax.fori_loop(0, nctx, shrink, 0, unroll=4)
    meet(nz, nctx)
    stage_in = inner_copies(nz, nctx, side, g_own, g_in, in_send, in_recv)
    for copy in stage_in:
        copy.start()
    down, up = edge_copies(
        nz, edge_out.at[0], edge_in.at[0], edge_out.at[1], edge_in.at[1], edge_send, edge_recv
    )

    @pl.when(z > 0)
    def _():
        down.start()

    @pl.when(z < nz - 1)
    def _():
        up.start()

    def oq_go(d, carry):
        plane_copy(
            nz, nctx, d, lambda p: oq_pack.at[p], lambda s: oq_all.at[s], oq_send, oq_recv
        ).start()
        return carry

    lax.fori_loop(1, nctx, oq_go, 0)
    oq_all[c] = oq_pack[c]

    total = g_own[...].astype(jnp.float32)
    for e, copy in enumerate(stage_in):
        copy.wait_recv()
        total = total + g_in[e + 1].astype(jnp.float32)
    g_mid[...] = total.astype(jnp.bfloat16)
    stage_out = outer_copies(nz, nctx, side, g_mid, g_out, out_send, out_recv)
    for copy in stage_out:
        copy.start()

    @pl.when(z > 0)
    def _():
        column_copy(
            jnp.maximum(z - 1, 0), edge_out.at[1], edge_in.at[1], edge_send.at[1], edge_recv.at[1]
        ).wait_recv()

    @pl.when(z == 0)
    def _():
        edge_in[1] = jnp.zeros_like(edge_in[1])

    @pl.when(z < nz - 1)
    def _():
        column_copy(
            jnp.minimum(z + 1, nz - 1), edge_out.at[0], edge_in.at[0], edge_send.at[0], edge_recv.at[0]
        ).wait_recv()

    @pl.when(z == nz - 1)
    def _():
        edge_in[0] = jnp.zeros_like(edge_in[0])

    for copy in stage_out:
        copy.wait_recv()
    for e in range(1, nz // side):
        total = total + g_out[e].astype(jnp.float32)
    wanted = [glob_ref[i] - z * local_blocks for i in range(GLOB)]

    def settle(j):
        for side_of in range(2):
            b = 2 * j + side_of
            term = sums_ref[pl.ds(pl.multiple_of((b + 1) * BLK, BLK), BLK), :].astype(jnp.float32)
            for i in range(GLOB):
                extra = total[i * BLK : (i + 1) * BLK]
                term = term + jnp.where(jnp.full(extra.shape, wanted[i] == b), extra, 0.0)
            edge = edge_in[1 - side_of].astype(jnp.float32)
            at_edge = j == (nctx - 1) * side_of
            term = term + jnp.where(jnp.full(edge.shape, at_edge), edge, 0.0)
            kv_pack[j, pl.ds(side_of * BLK, BLK), :] = term.astype(jnp.bfloat16)

    def kv_go(d, carry):
        settle(lax.rem(c + d, nctx))
        plane_copy(
            nz, nctx, d, lambda p: kv_pack.at[p], lambda s: kv_all.at[s], kv_send, kv_recv
        ).start()
        return carry

    lax.fori_loop(1, nctx, kv_go, 0)
    settle(c)
    kv_all[c] = kv_pack[c]

    all_of(oq_all.at[pl.ds(0, nctx - 1)], oq_send, oq_recv).wait_recv()
    all_of(kv_all.at[pl.ds(0, nctx - 1)], kv_send, kv_recv).wait_recv()
    all_of(oq_pack.at[pl.ds(0, nctx - 1)], oq_send, oq_recv).wait_send()
    all_of(kv_pack.at[pl.ds(0, nctx - 1)], kv_send, kv_recv).wait_send()

    @pl.when(z > 0)
    def _():
        down.wait_send()

    @pl.when(z < nz - 1)
    def _():
        up.wait_send()

    for copy in stage_in + stage_out:
        copy.wait_send()


def deliver(nz, nctx, rows, global_blocks, dqo, sums, rank):
    side = square(nz)
    half = jnp.bfloat16
    dma = pltpu.SemaphoreType.DMA
    vmem = pl.BlockSpec(memory_space=pltpu.VMEM)
    return pl.pallas_call(
        functools.partial(deliver_kernel, nz, nctx),
        out_shape=(
            jax.ShapeDtypeStruct((nctx, BLK + CAP // 2, 2 * HD), half),
            jax.ShapeDtypeStruct((nctx, rows, 2 * HD), half),
        ),
        in_specs=[pl.BlockSpec(memory_space=pltpu.SMEM)]
        + [pl.BlockSpec(memory_space=pl.ANY)] * 2
        + [vmem],
        out_specs=(vmem,) * 2,
        scratch_shapes=[
            pltpu.VMEM((nctx, BLK + CAP // 2, 2 * HD), half),
            pltpu.VMEM((nctx, rows, 2 * HD), half),
            pltpu.VMEM((2, BLK, 2 * HD), half),
            pltpu.VMEM((2, BLK, 2 * HD), half),
            pltpu.VMEM((GLOB * BLK, 2 * HD), half),
            pltpu.VMEM((side, GLOB * BLK, 2 * HD), half),
            pltpu.VMEM((GLOB * BLK, 2 * HD), half),
            pltpu.VMEM((nz // side, GLOB * BLK, 2 * HD), half),
            dma(()), dma(()), dma(()), dma(()),
            dma((2,)), dma((2,)),
            dma((side,)), dma((side,)), dma((nz // side,)), dma((nz // side,)),
            pltpu.VMEM(dqo.shape, half), pltpu.VMEM(sums.shape, half), dma((2,)),
        ],
        compiler_params=pltpu.CompilerParams(
            collective_id=1, has_side_effects=True, vmem_limit_bytes=56 * 1024 * 1024
        ),
        name="deliver",
    )(global_blocks, dqo, sums, rank)


def spread_kernel(oq_ref, kv_ref, rank_ref, most_ref, full_ref, o_ref, dq_ref, dk_ref, dv_ref, compact):
    few = CAP // 2
    for t in range(oq_ref.shape[0] // 2):
        columns = slice(2 * t * HD, 2 * (t + 1) * HD)
        first, second = oq_ref[2 * t], oq_ref[2 * t + 1]
        o_ref[:BLK, columns] = jnp.concatenate([first[:BLK, :HD], second[:BLK, :HD]], axis=1)
        o_ref[BLK:, columns] = jnp.concatenate([first[:BLK, HD:], second[:BLK, HD:]], axis=1)
        compact[:few, columns] = jnp.concatenate([first[BLK:, :HD], second[BLK:, :HD]], axis=1)
        compact[few:, columns] = jnp.concatenate([first[BLK:, HD:], second[BLK:, HD:]], axis=1)
        first, second = kv_ref[2 * t], kv_ref[2 * t + 1]
        dk_ref[:, columns] = jnp.concatenate([first[:, :HD], second[:, :HD]], axis=1)
        dv_ref[:, columns] = jnp.concatenate([first[:, HD:], second[:, HD:]], axis=1)
    marks = chosen(rank_ref[pl.ds(lax.axis_index("ctx"), 1), :])
    spread = contract(marks, compact[...], 0, 0).astype(jnp.bfloat16)
    crowded = jnp.full(spread.shape, most_ref[0, 0]) > CAP - 0.5
    dq_ref[...] = jnp.where(crowded, full_ref[...], spread)


def spread(oq, kv, rank, most, full):
    vmem = pl.BlockSpec(memory_space=pltpu.VMEM)
    return pl.pallas_call(
        spread_kernel,
        out_shape=(jax.ShapeDtypeStruct(full.shape, full.dtype),) * 4,
        in_specs=[vmem, vmem, vmem, pl.BlockSpec(memory_space=pltpu.SMEM), vmem],
        out_specs=(vmem,) * 4,
        scratch_shapes=[pltpu.VMEM((CAP, full.shape[1]), full.dtype)],
        compiler_params=pltpu.CompilerParams(vmem_limit_bytes=48 * 1024 * 1024),
        name="spread",
    )(oq, kv, rank, most, full)


def body(queries, keys, values, out_weight, cotangent, positions, global_blocks, random_blocks):
    rows_here = queries.shape[0]
    nz, nctx = lax.axis_size("fsdp"), lax.axis_size("ctx")
    local_blocks = nctx * rows_here // BLK
    kv, qg, rank, most = collect(
        nz, nctx, global_blocks, queries, keys, values, cotangent, out_weight, positions
    )
    crowded = most[0, 0] > CAP - 0.5

    def dense_gradient(qg):
        offset = (lax.axis_index("fsdp") * nctx + lax.axis_index("ctx")) * rows_here
        places = offset + jnp.arange(rows_here, dtype=jnp.int32)
        masked = jnp.any(positions[:, None] == places[None, :], axis=0)
        upstream = jnp.where(masked[:, None], cotangent, jnp.zeros_like(cotangent))
        weight = lax.all_gather(out_weight, "fsdp", axis=0, tiled=True)
        grad = contract(upstream, weight, 1, 1).astype(jnp.bfloat16)
        grad = lax.all_to_all(grad, "ctx", split_axis=1, concat_axis=0, tiled=True)
        return jnp.concatenate([qg[:, :HD], grad], axis=1)

    qg = lax.cond(crowded, dense_gradient, lambda qg: qg, qg)
    picks = random_blocks.transpose(2, 1, 0).reshape(random_blocks.shape[2], local_blocks)
    dqo, sums = attend(global_blocks, picks, kv, qg)
    parts, key_values = deliver(nz, nctx, rows_here, global_blocks, dqo, sums, rank)

    def dense_query():
        return lax.all_to_all(dqo[:, :HD], "ctx", split_axis=0, concat_axis=1, tiled=True)

    full = lax.cond(crowded, dense_query, lambda: jnp.zeros_like(queries))
    return spread(parts, key_values, rank, most, full)


def solution(mesh):
    split = P(("fsdp", "ctx"), None)
    return jax.shard_map(
        body,
        mesh=mesh,
        in_specs=(split, split, split, P("fsdp", None), split, P(), P(), P("fsdp", "ctx", None)),
        out_specs=(split, split, split, split),
        check_vma=False,
    )
```
